32 devices in a mesh: trace: 2 (over y), gx: 4 (over z), gy: 4 (over x, core).
Axes of the slice: x: 2, y: 2, z: 4, core: 2. Of those that a mesh axis runs over, the one named last changes fastest.
Arguments:
- traces: bfloat16 [8192, 4, 256], P(('trace', 'gx', 'gy')), may hold values from -4 to 4
- coupling: bfloat16 [8192, 4], P(('trace', 'gx', 'gy')), may hold values from 0.099609375 to 1.8984375
- tap_shift: int32 [8192], P(('trace', 'gx', 'gy')), may hold values from 0 to 63
- node_tile: int32 [8192, 1], P(('trace', 'gx', 'gy')), may hold values from 0 to 31; in each aligned block of 256 rows (0 to 255, 256 to 511, ...) at most 16 rows name the same one
- node_cell: int32 [8192], P(('trace', 'gx', 'gy')), may hold values from 0 to 524287
- field_prev: float32 [16, 1024, 1024], P('trace', 'gx', 'gy'), may hold values from -0.3125 to 0.3125
- field_now: float32 [16, 1024, 1024], P('trace', 'gx', 'gy'), may hold values from -0.3125 to 0.3125
- speed_sq: float32 [16, 1024, 1024], P('trace', 'gx', 'gy'), may hold values from 0.3 to 1
Outputs:
- out_prev: float32 [16, 1024, 1024], P('trace', 'gx', 'gy')
- out_now: float32 [16, 1024, 1024], P('trace', 'gx', 'gy')
The draws below stay inside these ranges and needn't reach their ends.
Inputs may be any that keep to these rules, and one draw needn't show every extreme that they name: `node_tile`: among the nodes of one device at most 16 lie in one tile, and some device has exactly 16 in some tile.
All inputs are finite; a program needn't handle non-finite values.
Results may differ from the reference program's by a relative error of at most 0.0003.
Values may be sent and summed in bfloat16 or wider, within the bound.
No kernel may reach another device: no remote copies, remote signals or barrier semaphores. Data moves between devices by JAX's collectives and lax.ppermute only.
A program may use at most 128 MiB of HBM per device.

```python
import math
import jax
import jax.numpy as jnp
import numpy as np
from jax import lax

CZ = 8
CX = 256
CY = 256
NODE_DEV = 256
NT = 256
STEPS = 4
COMP = 4
CAP = 16
RATE = 64
NODES = 8192
NZ = 16
NX = 1024
NY = 1024
N_GX = 4
N_GY = 4
DEVICES = 32


def touch_ends(entries, key, smallest, top_value):
    longest = entries.shape.index(max(entries.shape))
    spots = []
    for shift in (0, 1):
        where = [jax.random.randint(jax.random.fold_in(key, axis), (), 0, length) for axis, length in enumerate(entries.shape)]
        where[longest] = (where[longest] + shift) % entries.shape[longest]
        spots.append(tuple(where))
    return entries.at[spots[0]].set(smallest).at[spots[1]].set(top_value)


def steps_of(key, extent, cuts, least, top_value):
    gain, own = 1.0, jax.random.fold_in(key, 6)
    for position, shards_of in cuts:
        draws = jnp.exp(jax.random.uniform(jax.random.fold_in(own, position), (shards_of,), jnp.float32, least / len(cuts), top_value / len(cuts)))
        gain = gain * jnp.repeat(draws, extent[position] // shards_of).reshape([-1 if axis == position else 1 for axis in range(len(extent))])
    return gain


def shared_out(stream_key, own, number, rows, count, top, reach, lean):
    sequence = jax.random.permutation(stream_key, count)
    crowded, common = load_shares(count, rows * top, reach, lean, True), load_shares(count, rows * top, reach, lean, False)
    places = jnp.arange(count)

    def named(tallies, rotation):
        used = int((tallies > 0).sum())
        fixed = max(1, used // 4)
        moved = fixed + (places - fixed + rotation * (used - fixed)) % max(1, count - fixed)
        return jnp.zeros((count,), jnp.int32).at[sequence[jnp.where(places < fixed, places, moved)]].set(jnp.asarray(tallies, jnp.int32))

    tallies = jnp.where(number % 4 == 0, named(crowded, number // 4), named(common, number - number // 4 - 1))
    mixed = jax.random.permutation(jax.random.fold_in(own, 3), count)
    donor, receiver = mixed[0:count // 2 * 2:2], mixed[1:count // 2 * 2:2]
    margin = jnp.minimum(tallies[donor] - 1, reach - tallies[receiver]) // 2
    margin = jnp.where((donor == sequence[0]) | (receiver == sequence[0]) | (tallies[receiver] == 0), 0, jnp.maximum(margin, 0))
    moved = jax.random.randint(jax.random.fold_in(own, 4), (count // 2,), 0, 1 << 20) % (margin + 1)
    tallies = tallies.at[donor].add(-moved).at[receiver].add(moved)
    items = jnp.searchsorted(jnp.cumsum(tallies), jnp.arange(rows * top), side="right").astype(jnp.int32)
    listing = items.reshape(top, rows).T
    listing = listing[jax.random.permutation(jax.random.fold_in(own, 1), rows)]
    rotation = jax.random.randint(jax.random.fold_in(own, 2), (rows, 1), 0, top)
    return jnp.take_along_axis(listing, (jnp.arange(top)[None, :] + rotation) % top, axis=1)


def load_shares(count, total, reach, skew, full):
    weights = [(1 << 20) // math.isqrt(rank ** skew) + 1 for rank in range(1, count + 1)]
    largest = reach if full else min(reach, max(-(-total // count), total * weights[0] // sum(weights)))
    least = 1 if total - largest >= count - 1 else 0
    holding, rest = [largest] + [least] * (count - 1), total - largest - least * (count - 1)
    while rest > 0:
        free = [i for i in range(1, count) if holding[i] < largest] or [i for i in range(1, count) if holding[i] < reach]
        whole, left = sum([weights[i] for i in free]), rest
        for i in free:
            addition = min(reach - holding[i], max(1, left * weights[i] // whole), rest)
            holding[i] = holding[i] + addition
            rest = rest - addition
    return np.array(holding)


def scatter_about(key, extent, spread, most, cuts=(), kind=jnp.bfloat16):
    values = spread * jax.random.normal(key, extent, jnp.float32)
    if cuts:
        values = values * steps_of(key, extent, cuts, -0.22, 0.18)
    return jnp.clip(values, -most, most).astype(kind)


def setup_inputs(seed: int = 0) -> dict:
    arg_keys = jax.random.split(jax.random.key(seed), 9)
    traces = scatter_about(arg_keys[0], (NODES, COMP, NT), 0.25, 4.0, ((0, 32),))
    coupling = jnp.clip(1.0 + 0.18 * jax.random.normal(arg_keys[1], (NODES, COMP), jnp.float32), 0.099609375, 1.8984375).astype(jnp.bfloat16)
    tap_shift = touch_ends(jax.random.randint(arg_keys[2], (NODES,), 0, RATE), jax.random.fold_in(arg_keys[2], 1), 0, RATE - 1).astype(jnp.int32)
    node_tile_keys = jax.random.split(jax.random.fold_in(arg_keys[3], 1), NODES // NODE_DEV)
    node_tile_turns = jax.random.permutation(jax.random.fold_in(arg_keys[3], 3), NODES // NODE_DEV)
    node_tile = jax.vmap(lambda own, number: shared_out(jax.random.fold_in(arg_keys[3], 2), own, number, NODE_DEV, DEVICES, 1, CAP, 2))(node_tile_keys, node_tile_turns).reshape((NODES, 1))
    node_cell = touch_ends(jax.random.randint(arg_keys[4], (NODES,), 0, CZ * CX * CY), jax.random.fold_in(arg_keys[4], 1), 0, (CZ * CX * CY) - 1).astype(jnp.int32)
    field_prev = scatter_about(arg_keys[5], (NZ, NX, NY), ((CZ * CX * CY // NODE_DEV) ** -0.5), 0.3125, ((0, 2), (1, 4), (2, 4)), jnp.float32)
    field_now = scatter_about(arg_keys[6], (NZ, NX, NY), ((CZ * CX * CY // NODE_DEV) ** -0.5), 0.3125, ((0, 2), (1, 4), (2, 4)), jnp.float32)
    speed_sq = jnp.clip(0.3 + 0.7 * jax.random.uniform(arg_keys[7], (NZ, NX, NY), jnp.float32) ** steps_of(arg_keys[7], (NZ, NX, NY), ((0, 2), (1, 4), (2, 4)), -0.2, 0.2), 0.3, 1.0)
    return {"traces": traces, "coupling": coupling, "tap_shift": tap_shift, "node_tile": node_tile, "node_cell": node_cell, "field_prev": field_prev, "field_now": field_now, "speed_sq": speed_sq}


def make_kernel(shift_values):
    samples = jnp.arange(NT).astype(jnp.float32)
    step_numbers = jnp.arange(STEPS).astype(jnp.float32)
    centre = (NT - RATE // 2) - RATE * step_numbers[None, :] - shift_values.astype(jnp.float32)[:, None]
    offset = samples[None, None, :] - centre[:, :, None]
    window = 0.5 * (1.0 + jnp.cos(math.pi * offset / (2.0 * RATE)))
    inside = jnp.abs(offset) < 2.0 * RATE
    return jnp.where(inside, jnp.sinc(offset / RATE) * window, jnp.zeros_like(offset))


def resample(traces, coupling, shift_values):
    kernel = make_kernel(shift_values)
    combined = jnp.sum(traces.astype(jnp.float32) * coupling.astype(jnp.float32)[:, :, None], axis=1)
    return jnp.einsum("nt,nst->ns", combined, kernel, precision=lax.Precision.HIGHEST)


def laplace(field):
    padded = jnp.pad(field, 1)
    beside = padded[2:, 1:-1, 1:-1] + padded[:-2, 1:-1, 1:-1]
    beside = beside + padded[1:-1, 2:, 1:-1] + padded[1:-1, :-2, 1:-1]
    beside = beside + padded[1:-1, 1:-1, 2:] + padded[1:-1, 1:-1, :-2]
    return beside - 6.0 * field


def reference(traces, coupling, tap_shift, node_tile, node_cell, field_prev, field_now, speed_sq):
    amplitudes = resample(traces, coupling, tap_shift)
    tile_ids = node_tile[:, 0]
    slab_index = tile_ids // (N_GX * N_GY)
    first_tile = (tile_ids // N_GY) % N_GX
    second_tile = tile_ids % N_GY
    depth_cell = node_cell // (CX * CY)
    first_cell = (node_cell // CY) % CX
    second_cell = node_cell % CY
    global_index = ((slab_index * CZ + depth_cell) * NX + first_tile * CX + first_cell) * NY + second_tile * CY + second_cell
    global_index = global_index.astype(jnp.int32)
    for step_index in range(STEPS):
        source = jnp.zeros((NZ * NX * NY,), jnp.float32).at[global_index].add(amplitudes[:, step_index]).reshape(NZ, NX, NY)
        nextfield = 2.0 * field_now - field_prev + 0.25 * speed_sq * (laplace(field_now) + source)
        field_prev = field_now
        field_now = nextfield
    return field_prev, field_now
```

```python
import functools

import jax
import jax.numpy as jnp
import numpy as np
from jax import lax
from jax.experimental import pallas as pl
from jax.experimental.pallas import tpu as pltpu
from jax.sharding import PartitionSpec as P

NT = 256
STEPS = 4
RATE = 64
OFF = 16
GROUP = 16
SLOTS = 25
AXES = ("trace", "gx", "gy")
F32 = jnp.float32
BF16 = jnp.bfloat16
I32 = jnp.int32
I16 = jnp.int16
CODE_SCALES = (32767.0 / 0.3125, 32767.0 / 0.3125, 32767.0)
VMEM_LIMIT = 52 * 1024 * 1024


def log2(value):
    assert value & (value - 1) == 0
    return value.bit_length() - 1


def sinc_table():
    u = np.arange(NT)[None, :] + np.arange(STEPS * RATE)[:, None] - (NT - RATE // 2)
    u = u.astype(np.float64)
    table = np.sinc(u / RATE) * 0.5 * (1.0 + np.cos(np.pi * u / (2.0 * RATE)))
    return np.where(np.abs(u) < 2.0 * RATE, table, 0.0).astype(np.float32)


def vmem_spec():
    return pl.BlockSpec(memory_space=pltpu.VMEM)


def any_spec():
    return pl.BlockSpec(memory_space=pl.ANY)


def smem_spec():
    return pl.BlockSpec(memory_space=pltpu.SMEM)


def call(kernel, outs, in_specs, out_specs, scratch=(), bytes_accessed=0, flops=0):
    return pl.pallas_call(
        kernel,
        out_shape=outs,
        in_specs=in_specs,
        out_specs=out_specs,
        scratch_shapes=list(scratch),
        compiler_params=pltpu.CompilerParams(vmem_limit_bytes=VMEM_LIMIT),
        cost_estimate=pl.CostEstimate(
            flops=flops, bytes_accessed=bytes_accessed, transcendentals=0
        ),
    )


def coded(values, field):
    return jnp.round(values * CODE_SCALES[field]).astype(I32).astype(I16)


def decoded(codes, field):
    return codes.astype(I32).astype(F32) * (1.0 / CODE_SCALES[field])


def split3(values):
    first = values.astype(BF16).astype(F32)
    rest = values - first
    second = rest.astype(BF16).astype(F32)
    third = (rest - second).astype(BF16).astype(F32)
    return first, second, third


def amp_kernel(dims, traces_ref, coupling_ref, ints_ref, table_ref, out_ref, rank_ref, code_ref, msg_ref):
    nt, ngx, ngy, nz, nx, ny = dims
    count = nt * ngx * ngy
    nodes = traces_ref.shape[0]
    coupling = coupling_ref[...].astype(F32)
    combined = traces_ref[:, 0, :].astype(F32) * coupling[:, 0:1]
    for c in range(1, traces_ref.shape[1]):
        combined = combined + traces_ref[:, c, :].astype(F32) * coupling[:, c : c + 1]
    every = lax.dot_general(
        table_ref[...],
        combined,
        (((1,), (1,)), ((), ())),
        precision=lax.Precision.HIGHEST,
        preferred_element_type=F32,
    )
    shift = ints_ref[0:1, :]
    tile = ints_ref[1:2, :]
    cell = ints_ref[2:3, :]
    tap = lax.broadcasted_iota(I32, every.shape, 0) & (RATE - 1)
    chosen = jnp.where(tap == shift, every, 0.0)
    amps = jnp.concatenate(
        [
            jnp.sum(chosen[s * RATE : (s + 1) * RATE], axis=0, keepdims=True)
            for s in range(STEPS)
        ],
        axis=0,
    )
    gz = (tile >> log2(ngx * ngy)) * nz + (cell >> log2(nx * ny))
    gx = ((tile >> log2(ngy)) & (ngx - 1)) * nx + ((cell >> log2(ny)) & (nx - 1))
    gy = (tile & (ngy - 1)) * ny + (cell & (ny - 1))
    dest = lax.broadcasted_iota(I32, (count, nodes), 0)
    da = dest >> log2(ngx * ngy)
    lz = gz - da * nz
    lx = gx - ((dest >> log2(ngy)) & (ngx - 1)) * nx
    ly = gy - (dest & (ngy - 1)) * ny
    far = jnp.zeros((count, nodes), I32)
    for local, size in ((lz, nz), (lx, nx), (ly, ny)):
        far = far + jnp.maximum(-local, 0) + jnp.maximum(local - (size - 1), 0)
    held = far <= STEPS - 1
    plane = lz + da * (nz - 1 - 2 * lz) if nt == 2 else lz & 15
    code_ref[...] = ((plane << 18) + ((lx + OFF) << 9) + (ly + 8)).astype(F32)
    held_f = jnp.where(held, 1.0, 0.0)
    before = jnp.where(
        lax.broadcasted_iota(I32, (nodes, nodes), 0) < lax.broadcasted_iota(I32, (nodes, nodes), 1),
        1.0,
        0.0,
    )
    rank = jnp.dot(held_f.astype(BF16), before.astype(BF16), preferred_element_type=F32)
    rank_ref[...] = jnp.where(held, rank, -1000.0)
    counts = jnp.sum(held_f, axis=1, keepdims=True)

    lane_row = lax.broadcasted_iota(I32, (128, nodes), 0)
    slot = jnp.zeros((128, nodes), I32)
    for k in range(1, SLOTS):
        slot = slot + jnp.where(lane_row >= 5 * k, 1, 0)
    slot = jnp.where(lane_row >= 5 * SLOTS, -5000, slot).astype(F32)
    lanes = lax.broadcasted_iota(I32, (1, 128), 1)
    part = lanes
    for k in range(1, SLOTS + 1):
        part = part - jnp.where(lanes >= 5 * k, 5, 0)
    amp_parts = jnp.concatenate(list(split3(amps)) + [jnp.zeros((4, nodes), F32)], axis=0)
    sub = lax.broadcasted_iota(I32, (16, nodes), 0)

    def row_of(d, r):
        hit = jnp.where(slot == rank_ref[pl.ds(d, 1), :] - r * float(SLOTS), 1.0, 0.0)
        left = amp_parts
        for i, piece in enumerate(split3(code_ref[pl.ds(d, 1), :])):
            left = jnp.where(sub == 12 + i, piece, left)
        got = lax.dot_general(
            left.astype(BF16),
            hit.astype(BF16),
            (((1,), (1,)), ((), ())),
            preferred_element_type=F32,
        )
        value = got[12:13] + got[13:14] + got[14:15]
        for s in range(STEPS):
            value = jnp.where(part == s, got[s : s + 1] + got[4 + s : 5 + s] + got[8 + s : 9 + s], value)
        return value

    def first_row(d, _):
        msg_ref[0, pl.ds(d, 1), :] = row_of(d, 0)
        return 0

    lax.fori_loop(0, count, first_row, 0, unroll=4)
    head = msg_ref[0]
    lanes_all = lax.broadcasted_iota(I32, head.shape, 1)
    out_ref[:, 0:128] = jnp.where(lanes_all == 127, counts, head)
    out_ref[:, 128:] = jnp.zeros((count, out_ref.shape[1] - 128), F32)

    @pl.when(jnp.max(counts) > SLOTS)
    def _():
        for r in range(1, msg_ref.shape[0]):

            def next_row(d, _):
                msg_ref[r, pl.ds(d, 1), :] = row_of(d, r)
                return 0

            lax.fori_loop(0, count, next_row, 0)
            out_ref[:, r * 128 : (r + 1) * 128] = msg_ref[r]


def z_entries(nz):
    return (
        [(0, g) for g in range(1, STEPS + 1)]
        + [(1, g) for g in range(1, STEPS)]
        + [(2, g) for g in range(1, STEPS)]
    )


def edge_entries():
    return (
        [(0, g) for g in range(1, STEPS)]
        + [(1, g) for g in range(1, STEPS - 1)]
        + [(2, g) for g in range(1, STEPS - 1)]
    )


def sides_of(nt):
    return ("hi",) if nt == 2 else ("hi", "lo")


def own_plane(nt, side, g, nz):
    return nz - g if nt == 2 or side == "lo" else g - 1


def ghost_plane(side, g, nz):
    return nz - 1 + g if side == "hi" else 16 - g


def flipped(plane, flip, nz):
    return plane + flip * (nz - 1 - 2 * plane)


def planes_kernel(nt, info_ref, now_ref, prev_ref, speed_ref, *rest):
    outs, (buffer, sems) = rest[:-2], rest[-2:]
    nz = now_ref.shape[0]
    flip = info_ref[0]
    copies = []
    for i, side in enumerate(sides_of(nt)):
        for k, (field, g) in enumerate(z_entries(nz)):
            source = (now_ref, prev_ref, speed_ref)[field]
            z = flipped(own_plane(nt, side, g, nz), flip, nz)
            at = i * len(z_entries(nz)) + k
            copy = pltpu.make_async_copy(source.at[z], buffer.at[at], sems.at[at])
            copy.start()
            copies.append((copy, i, k, at, field))
    for copy, i, k, at, field in copies:
        copy.wait()
        outs[i][k] = coded(buffer[at], field)


def packed(acc, base, tiles, source, lanes):
    for j, tile in enumerate(tiles):
        start = base + 4 * j
        moved = pltpu.roll(tile, lax.rem(start - source + 128, 128), 1)
        acc = jnp.where((lanes >= start) & (lanes < start + 4), moved, acc)
    return acc


def strips_kernel(info_ref, now_ref, prev_ref, speed_ref, left_ref, right_ref, up_ref, down_ref):
    z = pl.program_id(0)
    nz = pl.num_programs(0)
    _, nx, ny = now_ref.shape
    base = GROUP * flipped(z, info_ref[0], nz)

    @pl.when(z == 0)
    def _():
        left_ref[...] = jnp.zeros_like(left_ref)
        right_ref[...] = jnp.zeros_like(right_ref)

    rows = 64
    lanes = lax.broadcasted_iota(I32, (rows, 128), 1)

    def chunk(k, _):
        at = pl.ds(pl.multiple_of(k * rows, rows), rows)
        fields = (now_ref, prev_ref, speed_ref)
        left_ref[at, :] = packed(left_ref[at, :], base, [f[0, at, 0:128] for f in fields], 0, lanes)
        right_ref[at, :] = packed(
            right_ref[at, :], base, [f[0, at, ny - 128 : ny] for f in fields], 124, lanes
        )
        return 0

    lax.fori_loop(0, nx // rows, chunk, 0)
    low = lax.broadcasted_iota(I32, (8, ny), 0) < 4
    up_ref[0, z] = jnp.where(low, pltpu.roll(prev_ref[0, nx - 8 : nx, :], 4, 0), now_ref[0, nx - 8 : nx, :])
    up_ref[1, z] = speed_ref[0, nx - 8 : nx, :]
    down_ref[0, z] = jnp.where(low, now_ref[0, 0:8, :], pltpu.roll(prev_ref[0, 0:8, :], 4, 0))
    down_ref[1, z] = speed_ref[0, 0:8, :]


def ghost_rows(ref, z, top):
    pair, speed = ref[0, z], ref[1, z]
    keep = lax.broadcasted_iota(I32, pair.shape, 0) < 4
    keep = jnp.logical_not(keep) if top else keep
    return (
        jnp.where(keep, pair, 0.0),
        jnp.where(keep, pltpu.roll(pair, 4, 0), 0.0),
        jnp.where(keep, speed, 0.0),
    )


def corners_kernel(info_ref, left_ref, right_ref, top_ref, bottom_ref, left_out, right_out):
    nx = left_ref.shape[0]
    nz, ny = top_ref.shape[1], top_ref.shape[3]
    lanes = lax.broadcasted_iota(I32, (8, 128), 1)
    for out, own, begin, source in ((left_out, left_ref, 0, 0), (right_out, right_ref, ny - 128, 124)):
        out[8 : 8 + nx, :] = own[...]
        for ref, top, row in ((top_ref, True, 0), (bottom_ref, False, 8 + nx)):
            acc = jnp.zeros((8, 128), F32)
            for z in range(nz):
                base = GROUP * flipped(z, info_ref[0], nz)
                tiles = [v[:, begin : begin + 128] for v in ghost_rows(ref, z, top)]
                acc = packed(acc, base, tiles, source, lanes)
            out[row : row + 8, :] = acc


def windows_kernel(nt, info_ref, left_ref, right_ref, from_left, from_right, top_ref, bottom_ref, own_ref, *outs):
    nz, ny = top_ref.shape[1], top_ref.shape[3]
    rows = left_ref.shape[0]
    step = 16
    lanes = lax.broadcasted_iota(I32, (step, 128), 1)
    inner = lanes & (GROUP - 1)

    def chunk(k, _):
        at = pl.ds(pl.multiple_of(k * step, step), step)
        parts = (from_left[at, :], left_ref[at, :], right_ref[at, :], from_right[at, :])
        windows = []
        for j in range(3):
            moved = [pltpu.roll(part, (4 * i - 4 * j) % 128, 1) for i, part in enumerate(parts)]
            window = jnp.where(
                inner < 4, moved[0], jnp.where(inner < 8, moved[1], jnp.where(inner < 12, moved[2], moved[3]))
            )
            own_ref[j, at, :] = window
            windows.append(window)
        for side, out in zip(sides_of(nt), outs):
            acc = jnp.zeros((step, 128), F32)
            for e, (field, g) in enumerate(edge_entries()):
                moved = pltpu.roll(windows[field], (GROUP * (e - own_plane(nt, side, g, nz))) % 128, 1)
                moved = moved * CODE_SCALES[field]
                acc = jnp.where((lanes >= GROUP * e) & (lanes < GROUP * (e + 1)), moved, acc)
            out[at, :] = jnp.round(acc).astype(I32).astype(I16)
        return 0

    lax.fori_loop(0, rows // step, chunk, 0)
    for side, out in zip(sides_of(nt), outs):
        for e, (field, g) in enumerate(edge_entries()):
            z = flipped(own_plane(nt, side, g, nz), info_ref[0], nz)
            both = jnp.concatenate(
                [ghost_rows(top_ref, z, True)[field], ghost_rows(bottom_ref, z, False)[field]], axis=0
            )
            both = coded(both, field)
            for t in range(ny // 128):
                row = rows + (e * (ny // 128) + t) * 16
                out[row : row + 16, :] = both[:, t * 128 : (t + 1) * 128]


def steps_kernel(nt, info_ref, now_hbm, prev_hbm, speed_hbm, msg_hbm, top_ref, bottom_ref, own_ref, *rest):
    sides = sides_of(nt)
    n_side = len(sides)
    planes_in, rest = rest[:n_side], rest[n_side:]
    edges_in, rest = rest[:n_side], rest[n_side:]
    out_prev, out_now = rest[:2]
    (a_ref, b_ref, c_ref, qa_ref, qb_ref, qc_ref, *rest) = rest[2:]
    src, rest = rest[:STEPS], rest[STEPS:]
    qsrc, rest = rest[:STEPS], rest[STEPS:]
    slots, counts, load_sems, msg_sem, store_sems = rest
    nz, nx, ny = now_hbm.shape
    rows = nx + 2 * OFF
    lots = a_ref.shape[0] // rows
    senders = msg_hbm.shape[0]
    flip = info_ref[0]

    msg_copy = pltpu.make_async_copy(msg_hbm.at[:, pl.ds(0, 128)], slots, msg_sem)
    msg_copy.start()
    loads = []
    for i, (field, ref) in enumerate(((now_hbm, a_ref), (prev_hbm, b_ref), (speed_hbm, c_ref))):
        for p in range(nz):
            copy = pltpu.make_async_copy(
                field.at[flipped(p, flip, nz)],
                ref.at[pl.ds(p * rows + OFF, nx), :],
                load_sems.at[i * nz + p],
            )
            copy.start()
            loads.append(copy)

    zero = jnp.zeros((rows, ny), F32)
    for ref in src:

        def clear(k, _):
            for t in range(ref.shape[0]):
                ref[t, pl.ds(pl.multiple_of(k * rows, 8), rows), :] = zero[:, 0:128]
            return 0

        lax.fori_loop(0, ref.shape[1] // rows, clear, 0)
    for ref in qsrc:
        ref[...] = jnp.zeros_like(ref)
    edge_zero = jnp.zeros((16, ny), F32)
    for ref in (a_ref, b_ref, c_ref):
        for p in range(lots):
            ref[p * rows : p * rows + 16, :] = edge_zero
            ref[p * rows + OFF + nx : (p + 1) * rows, :] = edge_zero
    if nt == 2:
        a_ref[(lots - 1) * rows : lots * rows, :] = zero
        b_ref[(lots - 1) * rows : lots * rows, :] = zero
    for p in range(nz):
        z = flipped(p, flip, nz)
        for ref, low, high in zip(
            (a_ref, b_ref, c_ref), ghost_rows(top_ref, z, True), ghost_rows(bottom_ref, z, False)
        ):
            ref[p * rows + 8 : p * rows + 16, :] = low
            ref[p * rows + OFF + nx : p * rows + OFF + nx + 8, :] = high
    for ref in (qa_ref, qb_ref, qc_ref):
        ref[...] = jnp.zeros_like(ref)
    erows = own_ref.shape[1]
    for j, ref in enumerate((qa_ref, qb_ref, qc_ref)):
        ref[8 : 8 + erows, 0:128] = own_ref[j]
    for side, planes, edges in zip(sides, planes_in, edges_in):
        for k, (field, g) in enumerate(z_entries(nz)):
            ref = (a_ref, b_ref, c_ref)[field]
            at = ghost_plane(side, g, nz) * rows
            ref[at + OFF : at + OFF + nx, :] = decoded(planes[k], field)
        strip = edges[0:erows, :].astype(I32).astype(F32)
        lanes = lax.broadcasted_iota(I32, strip.shape, 1)
        for e, (field, g) in enumerate(edge_entries()):
            p = ghost_plane(side, g, nz)
            at = p * rows
            ref = (a_ref, b_ref, c_ref)[field]
            for t in range(ny // 128):
                row = erows + (e * (ny // 128) + t) * 16
                both = decoded(edges[row : row + 16, :], field)
                ref[at + 8 : at + 16, t * 128 : (t + 1) * 128] = both[0:8]
                ref[at + OFF + nx : at + OFF + nx + 8, t * 128 : (t + 1) * 128] = both[8:16]
            qref = (qa_ref, qb_ref, qc_ref)[field]
            lot = p - 8
            moved = pltpu.roll(strip, (GROUP * (lot - e)) % 128, 1) * (1.0 / CODE_SCALES[field])
            inside = (lanes >= GROUP * lot) & (lanes < GROUP * (lot + 1))
            qref[8 : 8 + erows, 128:256] = jnp.where(inside, moved, qref[8 : 8 + erows, 128:256])

    lane = lax.broadcasted_iota(I32, (1, 128), 1)

    def place(d, k):
        code = slots[d, 5 * k + 4].astype(I32)
        p = code >> 18
        row = (code >> 9) & 511
        col = (code & 511) - 8
        t = jnp.clip(col >> 7, 0, ny // 128 - 1)
        at = pl.ds(p * rows + row, 1)
        hit = lane == col - t * 128
        for s in range(STEPS):
            src[s][t, at, :] = src[s][t, at, :] + jnp.where(hit, slots[d, 5 * k + s], 0.0)

        @pl.when((col < 4) | (col >= ny - 4))
        def _():
            qlane = GROUP * (p & 7) + jnp.where(col < 4, col + 4, col - (ny - 4) + 8)
            qhit = lane == qlane
            for s in range(STEPS):
                qsrc[s][p >> 3, pl.ds(row, 1), :] = qsrc[s][p >> 3, pl.ds(row, 1), :] + jnp.where(
                    qhit, slots[d, 5 * k + s], 0.0
                )

    def place_round(r):
        def sender(d, _):
            def one(k, _):
                place(d, k)
                return 0

            lax.fori_loop(0, jnp.clip(counts[d] - r * SLOTS, 0, SLOTS), one, 0)
            return 0

        lax.fori_loop(0, senders, sender, 0)

    msg_copy.wait()

    def count_one(d, most):
        count = slots[d, 127].astype(I32)
        counts[d] = count
        return jnp.maximum(most, count)

    most = lax.fori_loop(0, senders, count_one, 0)
    place_round(0)

    def extra(r, _):
        more = pltpu.make_async_copy(
            msg_hbm.at[:, pl.ds(pl.multiple_of(r * 128, 128), 128)], slots, msg_sem
        )
        more.start()
        more.wait()
        place_round(r)
        return 0

    lax.fori_loop(1, (most + SLOTS - 1) // SLOTS, extra, 0)
    for copy in loads:
        copy.wait()

    size = 16
    lanes = lax.broadcasted_iota(I32, (size, ny), 1)
    first, last = lanes == 0, lanes == ny - 1
    filler = [jnp.zeros((size, 128), F32)] * (ny // 128 - 2)

    def main_step(s, now, prev, qnow, after=None):
        more = STEPS - 1 - s
        begin = OFF - 8 if more else OFF
        chunks = (nx + 16 if more else nx) // size

        def plane(i, _):
            p = i if nt == 2 else (i - more + lots) & (lots - 1)
            base = p * rows
            above = lax.rem(p + 1, lots) * rows
            below = lax.rem(p + lots - 1, lots) * rows
            qtile = pl.ds(pl.multiple_of((p >> 3) * 128, 128), 128)
            group = GROUP * (p & 7)
            to_first = lax.rem(256 - 3 - group, 128)
            to_last = lax.rem(256 + 127 - 12 - group, 128)

            def chunk(k, _):
                r0 = pl.multiple_of(begin + k * size, 8)

                def part(ref, at, extra=0):
                    return ref[pl.ds(pl.multiple_of(at + r0 - extra, 8), size + 2 * extra), :]

                wide = part(now, base, 8)
                mid = wide[8 : 8 + size]
                q = qnow[pl.ds(r0, size), qtile]
                edge = jnp.concatenate(
                    [pltpu.roll(q, to_first, 1)] + filler + [pltpu.roll(q, to_last, 1)], axis=1
                )
                beside = part(now, above) + part(now, below)
                beside = beside + wide[7 : 7 + size] + wide[9 : 9 + size]
                beside = beside + jnp.where(first, edge, pltpu.roll(mid, 1, 1))
                beside = beside + jnp.where(last, edge, pltpu.roll(mid, ny - 1, 1))
                source = jnp.concatenate(
                    [
                        src[s][t, pl.ds(pl.multiple_of(base + r0, 8), size), :]
                        for t in range(ny // 128)
                    ],
                    axis=1,
                )
                result = (
                    2.0 * mid
                    - part(prev, base)
                    + (0.25 * part(c_ref, base)) * (beside - 6.0 * mid + source)
                )
                prev[pl.ds(pl.multiple_of(base + r0, 8), size), :] = result
                return 0

            lax.fori_loop(0, chunks, chunk, 0)
            if after is not None:
                after(i)
            return 0

        lax.fori_loop(0, nz + n_side * more, plane, 0)

    def q_step(s, now, prev):
        def chunk(k, _):
            r0 = pl.multiple_of(OFF - 8 + k * size, 8)
            wide = now[pl.ds(pl.multiple_of(r0 - 8, 8), size + 16), :]
            mid = wide[8 : 8 + size]
            beside = wide[7 : 7 + size] + wide[9 : 9 + size]
            for shift in (1, 255, GROUP, 256 - GROUP):
                beside = beside + pltpu.roll(mid, shift, 1)
            at = pl.ds(r0, size)
            source = jnp.concatenate([qsrc[s][0, at, :], qsrc[s][1, at, :]], axis=1)
            prev[at, :] = (
                2.0 * mid
                - prev[at, :]
                + (0.25 * qc_ref[at, :]) * (beside - 6.0 * mid + source)
            )
            return 0

        lax.fori_loop(0, (nx + 16) // size, chunk, 0)

    fields, windows = [a_ref, b_ref], [qa_ref, qb_ref]

    def store(ref, out, p, sem):
        return pltpu.make_async_copy(
            ref.at[pl.ds(p * rows + OFF, nx), :], out.at[flipped(p, flip, nz)], sem
        )

    for s in range(STEPS - 1):
        main_step(s, fields[0], fields[1], windows[0])
        q_step(s, windows[0], windows[1])
        fields, windows = fields[::-1], windows[::-1]
    for p in range(nz):
        store(fields[0], out_prev, p, store_sems.at[p]).start()

    def finish(p):
        store(fields[1], out_now, p, store_sems.at[nz + p]).start()

    main_step(STEPS - 1, fields[0], fields[1], windows[0], finish)
    for p in range(nz):
        store(fields[0], out_prev, p, store_sems.at[p]).wait()
        store(fields[1], out_now, p, store_sems.at[nz + p]).wait()


def shifted(value, axis, count, step):
    pairs = [(i, i + step) for i in range(count) if 0 <= i + step < count]
    return lax.ppermute(value, axis, pairs)


def to_depth(values, nt):
    if nt == 2:
        return [lax.ppermute(values[0], "trace", [(0, 1), (1, 0)])]
    return [shifted(values[0], "trace", nt, -1), shifted(values[1], "trace", nt, 1)]


def body(traces, coupling, tap_shift, node_tile, node_cell, field_prev, field_now, speed_sq):
    nt, ngx, ngy = (lax.axis_size(axis) for axis in AXES)
    count = nt * ngx * ngy
    nodes = traces.shape[0]
    nz, nx, ny = field_now.shape
    sides = len(sides_of(nt))
    assert nz + 2 * STEPS == 16 and ny == 256
    shape = jax.ShapeDtypeStruct
    flip = lax.axis_index("trace") if nt == 2 else jnp.int32(0)
    info = jnp.full((1,), flip, I32)
    fields = (field_now, field_prev, speed_sq)

    entries = len(z_entries(nz))
    plane_msgs = call(
        functools.partial(planes_kernel, nt),
        [shape((entries, nx, ny), I16)] * sides,
        [smem_spec()] + [any_spec()] * 3,
        [vmem_spec()] * sides,
        [pltpu.VMEM((sides * entries, nx, ny), F32), pltpu.SemaphoreType.DMA((sides * entries,))],
        bytes_accessed=sides * entries * nx * ny * 6,
    )(info, *fields)
    planes = to_depth(plane_msgs, nt)

    plane_spec = pl.BlockSpec((1, nx, ny), lambda z: (z, 0, 0))
    left, right, up, down = pl.pallas_call(
        strips_kernel,
        grid=(nz,),
        out_shape=[shape((nx, 128), F32)] * 2 + [shape((2, nz, 8, ny), F32)] * 2,
        in_specs=[smem_spec()] + [plane_spec] * 3,
        out_specs=[pl.BlockSpec((nx, 128), lambda z: (0, 0))] * 2
        + [pl.BlockSpec((2, nz, 8, ny), lambda z: (0, 0, 0, 0))] * 2,
        compiler_params=pltpu.CompilerParams(vmem_limit_bytes=VMEM_LIMIT),
        cost_estimate=pl.CostEstimate(
            flops=0, bytes_accessed=3 * nz * nx * ny * 4, transcendentals=0
        ),
    )(info, *fields)
    top = shifted(up, "gx", ngx, 1)
    bottom = shifted(down, "gx", ngx, -1)

    msg_rows = -(-nodes // SLOTS)
    ints = jnp.stack([tap_shift, node_tile[:, 0], node_cell])
    msg = call(
        functools.partial(amp_kernel, (nt, ngx, ngy, nz, nx, ny)),
        shape((count, msg_rows * 128), F32),
        [vmem_spec()] * 4,
        vmem_spec(),
        [pltpu.VMEM((count, nodes), F32)] * 2 + [pltpu.VMEM((msg_rows, count, 128), F32)],
        bytes_accessed=1 << 20,
        flops=1 << 30,
    )(traces, coupling, ints, jnp.asarray(sinc_table()))
    msg = msg.reshape(count, 1, msg_rows * 128)
    msg = lax.all_to_all(msg, AXES, split_axis=0, concat_axis=0, tiled=True)
    msg = msg.reshape(count, msg_rows * 128)

    erows = nx + 16
    left, right = call(
        corners_kernel,
        [shape((erows, 128), F32)] * 2,
        [smem_spec()] + [vmem_spec()] * 4,
        [vmem_spec()] * 2,
        bytes_accessed=1 << 20,
    )(info, left, right, top, bottom)
    from_left = shifted(right, "gy", ngy, 1)
    from_right = shifted(left, "gy", ngy, -1)

    edge_rows = erows + len(edge_entries()) * (ny // 128) * 16
    own, *edge_msgs = call(
        functools.partial(windows_kernel, nt),
        [shape((3, erows, 128), F32)] + [shape((edge_rows, 128), I16)] * sides,
        [smem_spec()] + [vmem_spec()] * 6,
        [vmem_spec()] * (1 + sides),
        bytes_accessed=1 << 20,
    )(info, left, right, from_left, from_right, top, bottom)
    edges = to_depth(edge_msgs, nt)

    rows = nx + 2 * OFF
    lots = nz + STEPS + 1 if nt == 2 else nz + 2 * STEPS
    source_lots = nz + STEPS - 1 if nt == 2 else lots
    out_prev, out_now = call(
        functools.partial(steps_kernel, nt),
        [shape((nz, nx, ny), F32)] * 2,
        [smem_spec()] + [any_spec()] * 4 + [vmem_spec()] * (3 + 2 * sides),
        [any_spec()] * 2,
        [pltpu.VMEM((lots * rows, ny), F32)] * 3
        + [pltpu.VMEM((rows, 256), F32)] * 3
        + [pltpu.VMEM((ny // 128, source_lots * rows, 128), F32)] * STEPS
        + [pltpu.VMEM((2, rows, 128), F32)] * STEPS
        + [
            pltpu.SMEM((count, 128), F32),
            pltpu.SMEM((count,), I32),
            pltpu.SemaphoreType.DMA((3 * nz,)),
            pltpu.SemaphoreType.DMA(()),
            pltpu.SemaphoreType.DMA((2 * nz,)),
        ],
        bytes_accessed=5 * nz * nx * ny * 4,
        flops=nz * nx * ny * STEPS * 16,
    )(info, *fields, msg, top, bottom, own, *planes, *edges)
    return out_prev, out_now


def solution(mesh):
    placed = (
        P(AXES, None, None),
        P(AXES, None),
        P(AXES),
        P(AXES, None),
        P(AXES),
        P("trace", "gx", "gy"),
        P("trace", "gx", "gy"),
        P("trace", "gx", "gy"),
    )
    return jax.shard_map(
        body,
        mesh=mesh,
        in_specs=placed,
        out_specs=(P("trace", "gx", "gy"), P("trace", "gx", "gy")),
        check_vma=False,
    )
```

```python
import functools

import jax
import jax.numpy as jnp
import numpy as np
from jax import lax
from jax.experimental import pallas as pl
from jax.experimental.pallas import tpu as pltpu
from jax.sharding import PartitionSpec as P

NT = 256
STEPS = 4
RATE = 64
OFF = 16
GROUP = 16
SLOTS = 128
BATCH = 16
AXES = ("trace", "gx", "gy")
F32 = jnp.float32
BF16 = jnp.bfloat16
I32 = jnp.int32
I16 = jnp.int16
CODE_SCALES = (32767.0 / 0.3125, 32767.0 / 0.3125, 32767.0)
VMEM_LIMIT = 52 * 1024 * 1024


def log2(value):
    assert value & (value - 1) == 0
    return value.bit_length() - 1


def sinc_table():
    u = np.arange(NT)[None, :] + np.arange(STEPS * RATE)[:, None] - (NT - RATE // 2)
    u = u.astype(np.float64)
    table = np.sinc(u / RATE) * 0.5 * (1.0 + np.cos(np.pi * u / (2.0 * RATE)))
    return np.where(np.abs(u) < 2.0 * RATE, table, 0.0).astype(np.float32)


def vmem_spec():
    return pl.BlockSpec(memory_space=pltpu.VMEM)


def any_spec():
    return pl.BlockSpec(memory_space=pl.ANY)


def smem_spec():
    return pl.BlockSpec(memory_space=pltpu.SMEM)


def call(kernel, outs, in_specs, out_specs, scratch=(), bytes_accessed=0, flops=0):
    return pl.pallas_call(
        kernel,
        out_shape=outs,
        in_specs=in_specs,
        out_specs=out_specs,
        scratch_shapes=list(scratch),
        compiler_params=pltpu.CompilerParams(vmem_limit_bytes=VMEM_LIMIT),
        cost_estimate=pl.CostEstimate(
            flops=flops, bytes_accessed=bytes_accessed, transcendentals=0
        ),
    )


def coded(values, field):
    return jnp.round(values * CODE_SCALES[field]).astype(I32).astype(I16)


def decoded(codes, field):
    return codes.astype(I32).astype(F32) * (1.0 / CODE_SCALES[field])


def split3(values):
    first = values.astype(BF16).astype(F32)
    rest = values - first
    second = rest.astype(BF16).astype(F32)
    third = (rest - second).astype(BF16).astype(F32)
    return first, second, third


def amp_kernel(dims, traces_ref, coupling_ref, ints_ref, table_ref, out_ref, rank_ref, code_ref, count_ref, near_ref):
    nt, ngx, ngy, nz, nx, ny = dims
    count = nt * ngx * ngy
    nodes = traces_ref.shape[0]
    coupling = coupling_ref[...].astype(F32)
    combined = traces_ref[:, 0, :].astype(F32) * coupling[:, 0:1]
    for c in range(1, traces_ref.shape[1]):
        combined = combined + traces_ref[:, c, :].astype(F32) * coupling[:, c : c + 1]
    every = lax.dot_general(
        table_ref[...],
        combined,
        (((1,), (1,)), ((), ())),
        precision=lax.Precision.HIGHEST,
        preferred_element_type=F32,
    )
    shift = ints_ref[0:1, :]
    tile = ints_ref[1:2, :]
    cell = ints_ref[2:3, :]
    tap = lax.broadcasted_iota(I32, every.shape, 0) & (RATE - 1)
    chosen = jnp.where(tap == shift, every, 0.0)
    amps = jnp.concatenate(
        [
            jnp.sum(chosen[s * RATE : (s + 1) * RATE], axis=0, keepdims=True)
            for s in range(STEPS)
        ],
        axis=0,
    )
    gz = (tile >> log2(ngx * ngy)) * nz + (cell >> log2(nx * ny))
    gx = ((tile >> log2(ngy)) & (ngx - 1)) * nx + ((cell >> log2(ny)) & (nx - 1))
    gy = (tile & (ngy - 1)) * ny + (cell & (ny - 1))
    dest = lax.broadcasted_iota(I32, (count, nodes), 0)
    da = dest >> log2(ngx * ngy)
    lz = gz - da * nz
    lx = gx - ((dest >> log2(ngy)) & (ngx - 1)) * nx
    ly = gy - (dest & (ngy - 1)) * ny
    far = jnp.zeros((count, nodes), I32)
    for local, size in ((lz, nz), (lx, nx), (ly, ny)):
        far = far + jnp.maximum(-local, 0) + jnp.maximum(local - (size - 1), 0)
    held = far <= STEPS - 1
    plane = lz + da * (nz - 1 - 2 * lz) if nt == 2 else lz & 15
    code_ref[...] = ((plane << 18) + ((lx + OFF) << 9) + (ly + 8)).astype(F32)
    near = held & ((ly < 4) | (ly >= ny - 4))
    held_f = jnp.where(held, 1.0, 0.0)
    near_f = jnp.where(near, 1.0, 0.0)
    before = jnp.where(
        lax.broadcasted_iota(I32, (nodes, nodes), 0) < lax.broadcasted_iota(I32, (nodes, nodes), 1),
        1.0,
        0.0,
    )
    both = jnp.concatenate([held_f, near_f], axis=0).astype(BF16)
    rank = jnp.dot(both, before.astype(BF16), preferred_element_type=F32)
    rank, near_rank = rank[:count], rank[count:]
    counts = jnp.sum(held_f, axis=1, keepdims=True)
    nears = jnp.sum(near_f, axis=1, keepdims=True)
    rank = jnp.where(near, near_rank, nears + rank - near_rank)
    rank_ref[...] = jnp.where(held, rank, -1000.0)
    count_ref[...] = jnp.broadcast_to(counts, count_ref.shape)
    near_ref[...] = jnp.broadcast_to(nears, near_ref.shape)

    slot = lax.broadcasted_iota(I32, (SLOTS, nodes), 0).astype(F32)
    sub = lax.broadcasted_iota(I32, (8, nodes), 0)
    row = lax.broadcasted_iota(I32, (8, SLOTS), 0)
    amp_parts = [jnp.concatenate([part, jnp.zeros_like(part)], axis=0) for part in split3(amps)]

    def tile_of(d, offset):
        hit = jnp.where(slot == rank_ref[pl.ds(d, 1), :] - offset, 1.0, 0.0)
        left = [
            jnp.where(sub == STEPS, code, part)
            for part, code in zip(amp_parts, split3(code_ref[pl.ds(d, 1), :]))
        ]
        got = lax.dot_general(
            jnp.concatenate(left, axis=0).astype(BF16),
            hit.astype(BF16),
            (((1,), (1,)), ((), ())),
            preferred_element_type=F32,
        )
        tile = jnp.where(row == STEPS + 1, count_ref[pl.ds(d, 1), :], got[0:8] + got[8:16] + got[16:24])
        return jnp.where(row == STEPS + 2, near_ref[pl.ds(d, 1), :], tile)

    out_ref[:, 8:, :] = jnp.zeros((count, out_ref.shape[1] - 8, SLOTS), F32)

    def first_tile(d, _):
        out_ref[d, 0:8, :] = tile_of(d, 0.0)
        return 0

    lax.fori_loop(0, count, first_tile, 0, unroll=8)

    @pl.when(jnp.max(counts) > SLOTS)
    def _():
        for r in range(1, out_ref.shape[1] // 8):

            def next_tile(d, _):
                out_ref[d, 8 * r : 8 * r + 8, :] = tile_of(d, r * float(SLOTS))
                return 0

            lax.fori_loop(0, count, next_tile, 0, unroll=8)


def z_entries(nz):
    return (
        [(0, g) for g in range(1, STEPS + 1)]
        + [(1, g) for g in range(1, STEPS)]
        + [(2, g) for g in range(1, STEPS)]
    )


def edge_entries():
    return (
        [(0, g) for g in range(1, STEPS)]
        + [(1, g) for g in range(1, STEPS - 1)]
        + [(2, g) for g in range(1, STEPS - 1)]
    )


def sides_of(nt):
    return ("hi",) if nt == 2 else ("hi", "lo")


def own_plane(nt, side, g, nz):
    return nz - g if nt == 2 or side == "lo" else g - 1


def ghost_plane(side, g, nz):
    return nz - 1 + g if side == "hi" else 16 - g


def flipped(plane, flip, nz):
    return plane + flip * (nz - 1 - 2 * plane)


def planes_kernel(nt, info_ref, now_ref, prev_ref, speed_ref, *rest):
    outs, (buffer, sems) = rest[:-2], rest[-2:]
    nz = now_ref.shape[0]
    flip = info_ref[0]
    copies = []
    for i, side in enumerate(sides_of(nt)):
        for k, (field, g) in enumerate(z_entries(nz)):
            source = (now_ref, prev_ref, speed_ref)[field]
            z = flipped(own_plane(nt, side, g, nz), flip, nz)
            at = i * len(z_entries(nz)) + k
            copy = pltpu.make_async_copy(source.at[z], buffer.at[at], sems.at[at])
            copy.start()
            copies.append((copy, i, k, at, field))
    for copy, i, k, at, field in copies:
        copy.wait()
        outs[i][k] = coded(buffer[at], field)


def packed(acc, base, tiles, source, lanes):
    for j, tile in enumerate(tiles):
        start = base + 4 * j
        moved = pltpu.roll(tile, lax.rem(start - source + 128, 128), 1)
        acc = jnp.where((lanes >= start) & (lanes < start + 4), moved, acc)
    return acc


def strips_kernel(
    info_ref, now_hbm, prev_hbm, speed_hbm, left_ref, right_ref, up_ref, down_ref, buffer, sems
):
    nz, nx, ny = now_hbm.shape
    flip = info_ref[0]
    copies = []
    for z in range(nz):
        for j, field in enumerate((now_hbm, prev_hbm, speed_hbm)):
            copy = pltpu.make_async_copy(field.at[z], buffer.at[j, z], sems.at[j, z])
            copy.start()
            copies.append(copy)
    left_ref[...] = jnp.zeros_like(left_ref)
    right_ref[...] = jnp.zeros_like(right_ref)
    rows = 64
    lanes = lax.broadcasted_iota(I32, (rows, 128), 1)
    low = lax.broadcasted_iota(I32, (8, ny), 0) < 4
    for z in range(nz):
        for copy in copies[3 * z : 3 * z + 3]:
            copy.wait()
        base = GROUP * flipped(z, flip, nz)
        for k in range(nx // rows):
            at = slice(k * rows, (k + 1) * rows)
            for ref, begin, source in ((left_ref, 0, 0), (right_ref, ny - 128, 124)):
                tiles = [buffer[j, z, at, begin : begin + 128] for j in range(3)]
                ref[at, :] = packed(ref[at, :], base, tiles, source, lanes)
        top, bottom = slice(nx - 8, nx), slice(0, 8)
        up_ref[0, z] = jnp.where(low, pltpu.roll(buffer[1, z, top, :], 4, 0), buffer[0, z, top, :])
        up_ref[1, z] = buffer[2, z, top, :]
        down_ref[0, z] = jnp.where(low, buffer[0, z, bottom, :], pltpu.roll(buffer[1, z, bottom, :], 4, 0))
        down_ref[1, z] = buffer[2, z, bottom, :]


def ghost_rows(ref, z, top):
    pair, speed = ref[0, z], ref[1, z]
    keep = lax.broadcasted_iota(I32, pair.shape, 0) < 4
    keep = jnp.logical_not(keep) if top else keep
    return (
        jnp.where(keep, pair, 0.0),
        jnp.where(keep, pltpu.roll(pair, 4, 0), 0.0),
        jnp.where(keep, speed, 0.0),
    )


def corners_kernel(info_ref, left_ref, right_ref, top_ref, bottom_ref, left_out, right_out):
    nx = left_ref.shape[0]
    nz, ny = top_ref.shape[1], top_ref.shape[3]
    lanes = lax.broadcasted_iota(I32, (8, 128), 1)
    for out, own, begin, source in ((left_out, left_ref, 0, 0), (right_out, right_ref, ny - 128, 124)):
        out[8 : 8 + nx, :] = own[...]
        for ref, top, row in ((top_ref, True, 0), (bottom_ref, False, 8 + nx)):
            acc = jnp.zeros((8, 128), F32)
            for z in range(nz):
                base = GROUP * flipped(z, info_ref[0], nz)
                tiles = [v[:, begin : begin + 128] for v in ghost_rows(ref, z, top)]
                acc = packed(acc, base, tiles, source, lanes)
            out[row : row + 8, :] = acc


def windows_kernel(nt, info_ref, left_ref, right_ref, from_left, from_right, top_ref, bottom_ref, own_ref, *outs):
    nz, ny = top_ref.shape[1], top_ref.shape[3]
    rows = left_ref.shape[0]
    step = 16
    lanes = lax.broadcasted_iota(I32, (step, 128), 1)
    inner = lanes & (GROUP - 1)

    def chunk(k, _):
        at = pl.ds(pl.multiple_of(k * step, step), step)
        parts = (from_left[at, :], left_ref[at, :], right_ref[at, :], from_right[at, :])
        windows = []
        for j in range(3):
            moved = [pltpu.roll(part, (4 * i - 4 * j) % 128, 1) for i, part in enumerate(parts)]
            window = jnp.where(
                inner < 4, moved[0], jnp.where(inner < 8, moved[1], jnp.where(inner < 12, moved[2], moved[3]))
            )
            own_ref[j, at, :] = window
            windows.append(window)
        for side, out in zip(sides_of(nt), outs):
            acc = jnp.zeros((step, 128), F32)
            for e, (field, g) in enumerate(edge_entries()):
                moved = pltpu.roll(windows[field], (GROUP * (e - own_plane(nt, side, g, nz))) % 128, 1)
                moved = moved * CODE_SCALES[field]
                acc = jnp.where((lanes >= GROUP * e) & (lanes < GROUP * (e + 1)), moved, acc)
            out[at, :] = jnp.round(acc).astype(I32).astype(I16)
        return 0

    lax.fori_loop(0, rows // step, chunk, 0, unroll=rows // step)
    for side, out in zip(sides_of(nt), outs):
        for e, (field, g) in enumerate(edge_entries()):
            z = flipped(own_plane(nt, side, g, nz), info_ref[0], nz)
            both = jnp.concatenate(
                [ghost_rows(top_ref, z, True)[field], ghost_rows(bottom_ref, z, False)[field]], axis=0
            )
            both = coded(both, field)
            for t in range(ny // 128):
                row = rows + (e * (ny // 128) + t) * 16
                out[row : row + 16, :] = both[:, t * 128 : (t + 1) * 128]


def steps_kernel(nt, info_ref, now_hbm, prev_hbm, speed_hbm, msg_hbm, top_hbm, bottom_hbm, own_hbm, *rest):
    sides = sides_of(nt)
    n_side = len(sides)
    planes_hbm, rest = rest[:n_side], rest[n_side:]
    edges_hbm, rest = rest[:n_side], rest[n_side:]
    out_prev, out_now = rest[:2]
    (a_ref, b_ref, c_ref, qa_ref, qb_ref, qc_ref, *rest) = rest[2:]
    planes_in, rest = rest[:n_side], rest[n_side:]
    edges_in, rest = rest[:n_side], rest[n_side:]
    src, qsrc, top_ref, bottom_ref, msg_ref, spots_ref, spots, in_sems, load_sems, store_sems = rest
    nz, nx, ny = now_hbm.shape
    rows = nx + 2 * OFF
    lots = a_ref.shape[0] // rows
    senders = msg_hbm.shape[0]
    flip = info_ref[0]

    def msg_copy(r):
        return pltpu.make_async_copy(msg_hbm.at[:, pl.ds(8 * r, 8), :], msg_ref, in_sems.at[0])

    def spots_copy():
        return pltpu.make_async_copy(spots_ref, spots, in_sems.at[1])

    def start(source, target, k):
        copy = pltpu.make_async_copy(source, target, in_sems.at[k])
        copy.start()
        return copy

    first_msg = msg_copy(0)
    first_msg.start()
    erows = own_hbm.shape[1]
    top_copies = [start(top_hbm, top_ref, 2), start(bottom_hbm, bottom_ref, 3)]
    own_copies = [
        start(own_hbm.at[j], ref.at[pl.ds(8, erows), pl.ds(0, 128)], 4 + j)
        for j, ref in enumerate((qa_ref, qb_ref, qc_ref))
    ]
    side_copies = [
        (start(planes_hbm[i], planes_in[i], 7 + 2 * i), start(edges_hbm[i], edges_in[i], 8 + 2 * i))
        for i in range(n_side)
    ]
    loads = []
    for i, (field, ref) in enumerate(((now_hbm, a_ref), (prev_hbm, b_ref), (speed_hbm, c_ref))):
        for p in range(nz):
            copy = pltpu.make_async_copy(
                field.at[flipped(p, flip, nz)],
                ref.at[pl.ds(p * rows + OFF, nx), :],
                load_sems.at[i * nz + p],
            )
            copy.start()
            loads.append(copy)

    source_lots = src.shape[0] // (2 * rows)
    flat = source_lots * rows
    zero = jnp.zeros((rows, 128), F32)
    zero4 = jnp.zeros((rows, STEPS, 128), F32)

    def clear_source(k, _):
        src[pl.ds(k * rows, rows), :, :] = zero4
        return 0

    lax.fori_loop(0, 2 * source_lots, clear_source, 0)
    for k in range(2):
        qsrc[pl.ds(k * rows, rows), :, :] = zero4

    def find_spots():
        code = msg_ref[:, STEPS, :].astype(I32)
        p = code >> 18
        row = (code >> 9) & 511
        col = (code & 511) - 8
        index = lax.broadcasted_iota(I32, code.shape, 1)
        used = code != 0
        t = jnp.clip(col >> 7, 0, ny // 128 - 1)
        inside = used & (col >= 0) & (col < ny)
        spare = (index & 1) * flat + ((index >> 1) & 7)
        at = jnp.where(inside, t * flat + p * rows + row, spare)
        turn = (col - t * 128 - index) & 127
        clash = jnp.zeros(code.shape, I32)
        for j in range(1, BATCH):
            same = (at == pltpu.roll(at, j, 1)) & ((index & (BATCH - 1)) >= j) & (index < 2 * BATCH)
            clash = clash | jnp.where(same, 1, 0)
        clash = jnp.max(clash, axis=1, keepdims=True)
        spots_ref[0] = (jnp.where(clash > 0, spare, at) << 7) + turn
        spots_ref[1] = (at << 7) + turn
        low = col < 4
        qlane = GROUP * (p & 7) + jnp.where(low, col + 4, col - (ny - 4) + 8)
        spots_ref[2] = (((p >> 3) * rows + row) << 7) + ((qlane - index) & 127)
        begin = jnp.where(clash > 0, 0, 2 * BATCH)
        counts = msg_ref[:, STEPS + 1, :].astype(I32)
        nears = msg_ref[:, STEPS + 2, :].astype(I32)
        spots_ref[3] = jnp.where(index == 0, counts, jnp.where(index == 1, nears, begin))

    first_msg.wait()
    find_spots()
    spots_copy().start()
    edge_zero = jnp.zeros((16, ny), F32)
    for ref in (a_ref, b_ref, c_ref):
        for p in range(lots):
            ref[p * rows : p * rows + 16, :] = edge_zero
            ref[p * rows + OFF + nx : (p + 1) * rows, :] = edge_zero
    if nt == 2:
        for ref in (a_ref, b_ref):
            for t in range(ny // 128):
                ref[(lots - 1) * rows : lots * rows, t * 128 : (t + 1) * 128] = zero
    for copy in top_copies:
        copy.wait()
    for p in range(nz):
        z = flipped(p, flip, nz)
        for ref, low, high in zip(
            (a_ref, b_ref, c_ref), ghost_rows(top_ref, z, True), ghost_rows(bottom_ref, z, False)
        ):
            ref[p * rows + 8 : p * rows + 16, :] = low
            ref[p * rows + OFF + nx : p * rows + OFF + nx + 8, :] = high
    for ref in (qa_ref, qb_ref, qc_ref):
        ref[0:8, 0:128] = jnp.zeros((8, 128), F32)
        ref[8 + erows :, 0:128] = jnp.zeros((rows - 8 - erows, 128), F32)
        ref[:, 128:256] = zero
    for side, planes, edges, copies in zip(sides, planes_in, edges_in, side_copies):
        for copy in copies:
            copy.wait()
        for k, (field, g) in enumerate(z_entries(nz)):
            ref = (a_ref, b_ref, c_ref)[field]
            at = ghost_plane(side, g, nz) * rows
            ref[at + OFF : at + OFF + nx, :] = decoded(planes[k], field)
        strip = edges[0:erows, :].astype(I32).astype(F32)
        lanes = lax.broadcasted_iota(I32, strip.shape, 1)
        for e, (field, g) in enumerate(edge_entries()):
            p = ghost_plane(side, g, nz)
            at = p * rows
            ref = (a_ref, b_ref, c_ref)[field]
            for t in range(ny // 128):
                row = erows + (e * (ny // 128) + t) * 16
                both = decoded(edges[row : row + 16, :], field)
                ref[at + 8 : at + 16, t * 128 : (t + 1) * 128] = both[0:8]
                ref[at + OFF + nx : at + OFF + nx + 8, t * 128 : (t + 1) * 128] = both[8:16]
            qref = (qa_ref, qb_ref, qc_ref)[field]
            lot = p - 8
            moved = pltpu.roll(strip, (GROUP * (lot - e)) % 128, 1) * (1.0 / CODE_SCALES[field])
            inside = (lanes >= GROUP * lot) & (lanes < GROUP * (lot + 1))
            qref[8 : 8 + erows, 128:256] = jnp.where(inside, moved, qref[8 : 8 + erows, 128:256])

    lane = lax.broadcasted_iota(I32, (8, 128), 1)

    def share(d, k, turn):
        one = jnp.where(lane == k, msg_ref[d], 0.0)
        return pltpu.roll(one, turn, 1)[0:STEPS]

    def place_batch(d, first):
        words = [spots[0, d, k] for k in range(first, first + BATCH)]
        tile = msg_ref[d]
        values = [
            src[word >> 7] + pltpu.roll(jnp.where(lane == first + k, tile, 0.0), word & 127, 1)[0:STEPS]
            for k, word in enumerate(words)
        ]
        for word, value in zip(words, values):
            src[word >> 7] = value

    def place_first(d, _):
        place_batch(d, 0)
        return 0

    def place_second(d, _):
        @pl.when(spots[3, d, 0] > BATCH)
        def _():
            place_batch(d, BATCH)

        return 0

    def place_rest(r):
        def sender(d, most):
            count = spots[3, d, 0]

            def one(k, _):
                word = spots[1, d, k]
                src[word >> 7] = src[word >> 7] + share(d, k, word & 127)
                return 0

            def window(k, _):
                word = spots[2, d, k]
                qsrc[word >> 7] = qsrc[word >> 7] + share(d, k, word & 127)
                return 0

            first = 0 if r is not None else spots[3, d, 2]
            done = 0 if r is None else r * SLOTS
            lax.fori_loop(first, jnp.clip(count - done, 0, SLOTS), one, 0)
            lax.fori_loop(0, jnp.clip(spots[3, d, 1] - done, 0, SLOTS), window, 0)
            return jnp.maximum(most, count)

        return lax.fori_loop(0, senders, sender, 0)

    spots_copy().wait()
    lax.fori_loop(0, senders, place_first, 0, unroll=4)
    lax.fori_loop(0, senders, place_second, 0)
    most = place_rest(None)

    def extra(r, _):
        again = msg_copy(r)
        again.start()
        again.wait()
        find_spots()
        again = spots_copy()
        again.start()
        again.wait()
        place_rest(r)
        return 0

    lax.fori_loop(1, (most + SLOTS - 1) // SLOTS, extra, 0)
    for copy in own_copies + loads:
        copy.wait()

    size = 16
    lanes = lax.broadcasted_iota(I32, (size, 128), 1)
    first, last = lanes == 0, lanes == 127

    def main_step(s, now, prev, qnow, after=None):
        more = STEPS - 1 - s
        begin = OFF - 8 if more else OFF
        chunks = (nx + 16 if more else nx) // size

        def plane(i, _):
            p = i if nt == 2 else (i - more + lots) & (lots - 1)
            base = p * rows
            above = lax.rem(p + 1, lots) * rows
            below = lax.rem(p + lots - 1, lots) * rows
            qtile = pl.ds(pl.multiple_of((p >> 3) * 128, 128), 128)
            group = GROUP * (p & 7)
            to_first = lax.rem(256 - 3 - group, 128)
            to_last = lax.rem(256 + 127 - 12 - group, 128)

            def chunk(k, _):
                r0 = pl.multiple_of(begin + k * size, 8)

                def part(ref, at, t, extra=0):
                    at = pl.ds(pl.multiple_of(at + r0 - extra, 8), size + 2 * extra)
                    return ref[at, t * 128 : (t + 1) * 128]

                q = qnow[pl.ds(r0, size), qtile]
                mids = [part(now, base, t) for t in range(2)]
                ahead = [pltpu.roll(mid, 1, 1) for mid in mids]
                behind = [pltpu.roll(mid, 127, 1) for mid in mids]
                left = [
                    jnp.where(first, pltpu.roll(q, to_first, 1), ahead[0]),
                    jnp.where(first, ahead[0], ahead[1]),
                ]
                right = [
                    jnp.where(last, behind[1], behind[0]),
                    jnp.where(last, pltpu.roll(q, to_last, 1), behind[1]),
                ]
                for t in range(2):
                    wide = part(now, base, t, 8)
                    mid = mids[t]
                    beside = part(now, above, t) + part(now, below, t)
                    beside = beside + (wide[7 : 7 + size] + wide[9 : 9 + size])
                    beside = beside + (left[t] + right[t])
                    source = src[pl.ds(pl.multiple_of(t * flat + base + r0, 8), size), s, :]
                    result = (
                        2.0 * mid
                        - part(prev, base, t)
                        + (0.25 * part(c_ref, base, t)) * (beside - 6.0 * mid + source)
                    )
                    at = pl.ds(pl.multiple_of(base + r0, 8), size)
                    prev[at, t * 128 : (t + 1) * 128] = result
                return 0

            lax.fori_loop(0, chunks, chunk, 0, unroll=chunks)
            if after is not None:
                after(i)
            return 0

        lax.fori_loop(0, nz + n_side * more, plane, 0, unroll=True)

    def q_step(s, now, prev):
        def chunk(k, _):
            r0 = pl.multiple_of(OFF - 8 + k * size, 8)
            wide = now[pl.ds(pl.multiple_of(r0 - 8, 8), size + 16), :]
            mid = wide[8 : 8 + size]
            beside = wide[7 : 7 + size] + wide[9 : 9 + size]
            for shift in (1, 255, GROUP, 256 - GROUP):
                beside = beside + pltpu.roll(mid, shift, 1)
            at = pl.ds(r0, size)
            source = jnp.concatenate(
                [qsrc[pl.ds(r0, size), s, :], qsrc[pl.ds(rows + r0, size), s, :]], axis=1
            )
            prev[at, :] = (
                2.0 * mid
                - prev[at, :]
                + (0.25 * qc_ref[at, :]) * (beside - 6.0 * mid + source)
            )
            return 0

        lax.fori_loop(0, (nx + 16) // size, chunk, 0, unroll=(nx + 16) // size)

    fields, windows = [a_ref, b_ref], [qa_ref, qb_ref]

    def store(ref, out, p, sem):
        return pltpu.make_async_copy(
            ref.at[pl.ds(p * rows + OFF, nx), :], out.at[flipped(p, flip, nz)], sem
        )

    for s in range(STEPS - 1):
        main_step(s, fields[0], fields[1], windows[0])
        q_step(s, windows[0], windows[1])
        fields, windows = fields[::-1], windows[::-1]
    for p in range(nz):
        store(fields[0], out_prev, p, store_sems.at[p]).start()

    def finish(p):
        store(fields[1], out_now, p, store_sems.at[nz + p]).start()

    main_step(STEPS - 1, fields[0], fields[1], windows[0], finish)
    for p in range(nz):
        store(fields[0], out_prev, p, store_sems.at[p]).wait()
        store(fields[1], out_now, p, store_sems.at[nz + p]).wait()


def shifted(value, axis, count, step):
    pairs = [(i, i + step) for i in range(count) if 0 <= i + step < count]
    return lax.ppermute(value, axis, pairs)


def to_depth(values, nt):
    if nt == 2:
        return [lax.ppermute(values[0], "trace", [(0, 1), (1, 0)])]
    return [shifted(values[0], "trace", nt, -1), shifted(values[1], "trace", nt, 1)]


def body(traces, coupling, tap_shift, node_tile, node_cell, field_prev, field_now, speed_sq):
    nt, ngx, ngy = (lax.axis_size(axis) for axis in AXES)
    count = nt * ngx * ngy
    nodes = traces.shape[0]
    nz, nx, ny = field_now.shape
    sides = len(sides_of(nt))
    assert nz + 2 * STEPS == 16 and ny == 256
    shape = jax.ShapeDtypeStruct
    flip = lax.axis_index("trace") if nt == 2 else jnp.int32(0)
    info = jnp.full((1,), flip, I32)
    fields = (field_now, field_prev, speed_sq)

    entries = len(z_entries(nz))
    plane_msgs = call(
        functools.partial(planes_kernel, nt),
        [shape((entries, nx, ny), I16)] * sides,
        [smem_spec()] + [any_spec()] * 3,
        [vmem_spec()] * sides,
        [pltpu.VMEM((sides * entries, nx, ny), F32), pltpu.SemaphoreType.DMA((sides * entries,))],
        bytes_accessed=sides * entries * nx * ny * 6,
    )(info, *fields)
    planes = to_depth(plane_msgs, nt)

    left, right, up, down = call(
        strips_kernel,
        [shape((nx, 128), F32)] * 2 + [shape((2, nz, 8, ny), F32)] * 2,
        [smem_spec()] + [any_spec()] * 3,
        [vmem_spec()] * 4,
        [pltpu.VMEM((3, nz, nx, ny), F32), pltpu.SemaphoreType.DMA((3, nz))],
        bytes_accessed=3 * nz * nx * ny * 4,
    )(info, *fields)
    top = shifted(up, "gx", ngx, 1)
    bottom = shifted(down, "gx", ngx, -1)

    rounds = -(-nodes // SLOTS)
    ints = jnp.stack([tap_shift, node_tile[:, 0], node_cell])
    msg = call(
        functools.partial(amp_kernel, (nt, ngx, ngy, nz, nx, ny)),
        shape((count, 8 * rounds, SLOTS), F32),
        [vmem_spec()] * 4,
        vmem_spec(),
        [pltpu.VMEM((count, nodes), F32)] * 2 + [pltpu.VMEM((count, SLOTS), F32)] * 2,
        bytes_accessed=1 << 20,
        flops=1 << 30,
    )(traces, coupling, ints, jnp.asarray(sinc_table()))
    msg, top, bottom = lax.optimization_barrier((msg, top, bottom))
    msg = lax.all_to_all(msg, AXES, split_axis=0, concat_axis=0, tiled=True)

    erows = nx + 16
    left, right = call(
        corners_kernel,
        [shape((erows, 128), F32)] * 2,
        [smem_spec()] + [vmem_spec()] * 4,
        [vmem_spec()] * 2,
        bytes_accessed=1 << 20,
    )(info, left, right, top, bottom)
    from_left = shifted(right, "gy", ngy, 1)
    from_right = shifted(left, "gy", ngy, -1)

    edge_rows = erows + len(edge_entries()) * (ny // 128) * 16
    own, *edge_msgs = call(
        functools.partial(windows_kernel, nt),
        [shape((3, erows, 128), F32)] + [shape((edge_rows, 128), I16)] * sides,
        [smem_spec()] + [vmem_spec()] * 6,
        [vmem_spec()] * (1 + sides),
        bytes_accessed=1 << 20,
    )(info, left, right, from_left, from_right, top, bottom)
    edges = to_depth(edge_msgs, nt)

    rows = nx + 2 * OFF
    lots = nz + STEPS + 1 if nt == 2 else nz + 2 * STEPS
    source_lots = nz + STEPS - 1 if nt == 2 else lots
    out_prev, out_now = call(
        functools.partial(steps_kernel, nt),
        [shape((nz, nx, ny), F32)] * 2,
        [smem_spec()] + [any_spec()] * (7 + 2 * sides),
        [any_spec()] * 2,
        [pltpu.VMEM((lots * rows, ny), F32)] * 3
        + [pltpu.VMEM((rows, 256), F32)] * 3
        + [pltpu.VMEM((entries, nx, ny), I16)] * sides
        + [pltpu.VMEM((edge_rows, 128), I16)] * sides
        + [
            pltpu.VMEM((2 * source_lots * rows, STEPS, 128), F32),
            pltpu.VMEM((2 * rows, STEPS, 128), F32),
            pltpu.VMEM((2, nz, 8, ny), F32),
            pltpu.VMEM((2, nz, 8, ny), F32),
            pltpu.VMEM((count, 8, SLOTS), F32),
            pltpu.VMEM((4, count, SLOTS), I32),
            pltpu.SMEM((4, count, SLOTS), I32),
            pltpu.SemaphoreType.DMA((7 + 2 * sides,)),
            pltpu.SemaphoreType.DMA((3 * nz,)),
            pltpu.SemaphoreType.DMA((2 * nz,)),
        ],
        bytes_accessed=5 * nz * nx * ny * 4,
        flops=nz * nx * ny * STEPS * 16,
    )(info, *fields, msg, top, bottom, own, *planes, *edges)
    return out_prev, out_now


def solution(mesh):
    placed = (
        P(AXES, None, None),
        P(AXES, None),
        P(AXES),
        P(AXES, None),
        P(AXES),
        P("trace", "gx", "gy"),
        P("trace", "gx", "gy"),
        P("trace", "gx", "gy"),
    )
    return jax.shard_map(
        body,
        mesh=mesh,
        in_specs=placed,
        out_specs=(P("trace", "gx", "gy"), P("trace", "gx", "gy")),
        check_vma=False,
    )
```

```python
import functools

import jax
import jax.numpy as jnp
import numpy as np
from jax import lax
from jax.experimental import pallas as pl
from jax.experimental.pallas import tpu as pltpu
from jax.sharding import PartitionSpec as P

NT = 256
STEPS = 4
RATE = 64
OFF = 16
GROUP = 16
SLOTS = 128
BATCH = 16
AXES = ("trace", "gx", "gy")
F32 = jnp.float32
BF16 = jnp.bfloat16
I32 = jnp.int32
I16 = jnp.int16
CODE_SCALES = (32767.0 / 0.3125, 32767.0 / 0.3125, 32767.0)
VMEM_LIMIT = 52 * 1024 * 1024
SMALL_LIMIT = 8 * 1024 * 1024


def log2(value):
    assert value & (value - 1) == 0
    return value.bit_length() - 1


def sinc_table():
    u = np.arange(NT)[None, :] + np.arange(STEPS * RATE)[:, None] - (NT - RATE // 2)
    u = u.astype(np.float64)
    table = np.sinc(u / RATE) * 0.5 * (1.0 + np.cos(np.pi * u / (2.0 * RATE)))
    return np.where(np.abs(u) < 2.0 * RATE, table, 0.0).astype(np.float32)


def vmem_spec():
    return pl.BlockSpec(memory_space=pltpu.VMEM)


def any_spec():
    return pl.BlockSpec(memory_space=pl.ANY)


def smem_spec():
    return pl.BlockSpec(memory_space=pltpu.SMEM)


def call(
    kernel, outs, in_specs, out_specs, scratch=(), bytes_accessed=0, flops=0, aliases=None,
    limit=VMEM_LIMIT
):
    return pl.pallas_call(
        kernel,
        out_shape=outs,
        in_specs=in_specs,
        out_specs=out_specs,
        scratch_shapes=list(scratch),
        input_output_aliases=aliases or {},
        compiler_params=pltpu.CompilerParams(vmem_limit_bytes=limit),
        cost_estimate=pl.CostEstimate(
            flops=flops, bytes_accessed=bytes_accessed, transcendentals=0
        ),
    )


def coded(values, field):
    return jnp.round(values * CODE_SCALES[field]).astype(I32).astype(I16)


def decoded(codes, field):
    return codes.astype(I32).astype(F32) * (1.0 / CODE_SCALES[field])


def in_hbm(*values):
    return [pltpu.with_memory_space_constraint(value, pltpu.HBM) for value in values]


def split3(values):
    first = values.astype(BF16).astype(F32)
    rest = values - first
    second = rest.astype(BF16).astype(F32)
    third = (rest - second).astype(BF16).astype(F32)
    return first, second, third


def amp_kernel(
    dims, traces_hbm, coupling_ref, ints_ref, table_hbm, out_ref,
    rank_ref, code_ref, count_ref, near_ref, traces_ref, table_ref, sems,
):
    nt, ngx, ngy, nz, nx, ny = dims
    count = nt * ngx * ngy
    nodes = traces_ref.shape[0]
    traces_copy = pltpu.make_async_copy(traces_hbm, traces_ref, sems.at[0])
    table_copy = pltpu.make_async_copy(table_hbm, table_ref, sems.at[1])
    traces_copy.start()
    table_copy.start()
    shift = ints_ref[0:1, :]
    tile = ints_ref[1:2, :]
    cell = ints_ref[2:3, :]
    gz = (tile >> log2(ngx * ngy)) * nz + (cell >> log2(nx * ny))
    gx = ((tile >> log2(ngy)) & (ngx - 1)) * nx + ((cell >> log2(ny)) & (nx - 1))
    gy = (tile & (ngy - 1)) * ny + (cell & (ny - 1))
    dest = lax.broadcasted_iota(I32, (count, nodes), 0)
    da = dest >> log2(ngx * ngy)
    lz = gz - da * nz
    lx = gx - ((dest >> log2(ngy)) & (ngx - 1)) * nx
    ly = gy - (dest & (ngy - 1)) * ny
    far = jnp.zeros((count, nodes), I32)
    for local, size in ((lz, nz), (lx, nx), (ly, ny)):
        far = far + jnp.maximum(-local, 0) + jnp.maximum(local - (size - 1), 0)
    held = far <= STEPS - 1
    plane = lz + da * (nz - 1 - 2 * lz) if nt == 2 else lz & 15
    code_ref[...] = ((plane << 18) + ((lx + OFF) << 9) + (ly + 8)).astype(F32)
    near = held & ((ly < 4) | (ly >= ny - 4))
    held_f = jnp.where(held, 1.0, 0.0)
    near_f = jnp.where(near, 1.0, 0.0)
    before = jnp.where(
        lax.broadcasted_iota(I32, (nodes, nodes), 0) < lax.broadcasted_iota(I32, (nodes, nodes), 1),
        1.0,
        0.0,
    )
    both = jnp.concatenate([held_f, near_f], axis=0).astype(BF16)
    rank = jnp.dot(both, before.astype(BF16), preferred_element_type=F32)
    rank, near_rank = rank[:count], rank[count:]
    counts = jnp.sum(held_f, axis=1, keepdims=True)
    nears = jnp.sum(near_f, axis=1, keepdims=True)
    rank = jnp.where(near, near_rank, nears + rank - near_rank)
    rank_ref[...] = jnp.where(held, rank, -1000.0)
    count_ref[...] = jnp.broadcast_to(counts, count_ref.shape)
    near_ref[...] = jnp.broadcast_to(nears, near_ref.shape)

    slot = lax.broadcasted_iota(I32, (SLOTS, nodes), 0).astype(F32)
    sub = lax.broadcasted_iota(I32, (8, nodes), 0)
    row = lax.broadcasted_iota(I32, (8, SLOTS), 0)
    traces_copy.wait()
    table_copy.wait()
    coupling = coupling_ref[...].astype(F32)
    combined = traces_ref[:, 0, :].astype(F32) * coupling[:, 0:1]
    for c in range(1, traces_ref.shape[1]):
        combined = combined + traces_ref[:, c, :].astype(F32) * coupling[:, c : c + 1]
    every = lax.dot_general(
        table_ref[...],
        combined,
        (((1,), (1,)), ((), ())),
        precision=lax.Precision.HIGHEST,
        preferred_element_type=F32,
    )
    tap = lax.broadcasted_iota(I32, every.shape, 0) & (RATE - 1)
    chosen = jnp.where(tap == shift, every, 0.0)
    amps = jnp.concatenate(
        [
            jnp.sum(chosen[s * RATE : (s + 1) * RATE], axis=0, keepdims=True)
            for s in range(STEPS)
        ],
        axis=0,
    )
    amp_parts = [jnp.concatenate([part, jnp.zeros_like(part)], axis=0) for part in split3(amps)]

    def tile_of(d, offset):
        hit = jnp.where(slot == rank_ref[pl.ds(d, 1), :] - offset, 1.0, 0.0)
        left = [
            jnp.where(sub == STEPS, code, part)
            for part, code in zip(amp_parts, split3(code_ref[pl.ds(d, 1), :]))
        ]
        got = lax.dot_general(
            jnp.concatenate(left, axis=0).astype(BF16),
            hit.astype(BF16),
            (((1,), (1,)), ((), ())),
            preferred_element_type=F32,
        )
        tile = jnp.where(row == STEPS + 1, count_ref[pl.ds(d, 1), :], got[0:8] + got[8:16] + got[16:24])
        return jnp.where(row == STEPS + 2, near_ref[pl.ds(d, 1), :], tile)

    out_ref[:, 8:, :] = jnp.zeros((count, out_ref.shape[1] - 8, SLOTS), F32)

    def first_tile(d, _):
        out_ref[d, 0:8, :] = tile_of(d, 0.0)
        return 0

    lax.fori_loop(0, count, first_tile, 0, unroll=8)

    @pl.when(jnp.max(counts) > SLOTS)
    def _():
        for r in range(1, out_ref.shape[1] // 8):

            def next_tile(d, _):
                out_ref[d, 8 * r : 8 * r + 8, :] = tile_of(d, r * float(SLOTS))
                return 0

            lax.fori_loop(0, count, next_tile, 0, unroll=8)


def z_entries(nz):
    return (
        [(0, g) for g in range(1, STEPS + 1)]
        + [(1, g) for g in range(1, STEPS)]
        + [(2, g) for g in range(1, STEPS)]
    )


def edge_entries():
    return (
        [(0, g) for g in range(1, STEPS)]
        + [(1, g) for g in range(1, STEPS - 1)]
        + [(2, g) for g in range(1, STEPS - 1)]
    )


def sides_of(nt):
    return ("hi",) if nt == 2 else ("hi", "lo")


def own_plane(nt, side, g, nz):
    return nz - g if nt == 2 or side == "lo" else g - 1


def ghost_plane(side, g, nz):
    return nz - 1 + g if side == "hi" else 16 - g


def flipped(plane, flip, nz):
    return plane + flip * (nz - 1 - 2 * plane)


def planes_kernel(nt, info_ref, now_ref, prev_ref, speed_ref, *rest):
    outs, (buffer, sems) = rest[:-2], rest[-2:]
    nz = now_ref.shape[0]
    flip = info_ref[0]
    copies = []
    for i, side in enumerate(sides_of(nt)):
        for k, (field, g) in enumerate(z_entries(nz)):
            source = (now_ref, prev_ref, speed_ref)[field]
            z = flipped(own_plane(nt, side, g, nz), flip, nz)
            at = i * len(z_entries(nz)) + k
            copy = pltpu.make_async_copy(source.at[z], buffer.at[at], sems.at[at])
            copy.start()
            copies.append((copy, i, k, at, field))
    for copy, i, k, at, field in copies:
        copy.wait()
        outs[i][k] = coded(buffer[at], field)


def packed(acc, base, tiles, source, lanes):
    for j, tile in enumerate(tiles):
        start = base + 4 * j
        moved = pltpu.roll(tile, lax.rem(start - source + 128, 128), 1)
        acc = jnp.where((lanes >= start) & (lanes < start + 4), moved, acc)
    return acc


def strips_kernel(
    info_ref, now_hbm, prev_hbm, speed_hbm, left_ref, right_ref, up_ref, down_ref, buffer, sems
):
    nz, nx, ny = now_hbm.shape
    flip = info_ref[0]
    copies = []
    for z in range(nz):
        for j, field in enumerate((now_hbm, prev_hbm, speed_hbm)):
            copy = pltpu.make_async_copy(field.at[z], buffer.at[j, z], sems.at[j, z])
            copy.start()
            copies.append(copy)
    left_ref[...] = jnp.zeros_like(left_ref)
    right_ref[...] = jnp.zeros_like(right_ref)
    rows = 64
    lanes = lax.broadcasted_iota(I32, (rows, 128), 1)
    low = lax.broadcasted_iota(I32, (8, ny), 0) < 4
    for z in range(nz):
        for copy in copies[3 * z : 3 * z + 3]:
            copy.wait()
        base = GROUP * flipped(z, flip, nz)
        for k in range(nx // rows):
            at = slice(k * rows, (k + 1) * rows)
            for ref, begin, source in ((left_ref, 0, 0), (right_ref, ny - 128, 124)):
                tiles = [buffer[j, z, at, begin : begin + 128] for j in range(3)]
                ref[at, :] = packed(ref[at, :], base, tiles, source, lanes)
        top, bottom = slice(nx - 8, nx), slice(0, 8)
        up_ref[0, z] = jnp.where(low, pltpu.roll(buffer[1, z, top, :], 4, 0), buffer[0, z, top, :])
        up_ref[1, z] = buffer[2, z, top, :]
        down_ref[0, z] = jnp.where(low, buffer[0, z, bottom, :], pltpu.roll(buffer[1, z, bottom, :], 4, 0))
        down_ref[1, z] = buffer[2, z, bottom, :]


def ghost_rows(ref, z, top):
    pair, speed = ref[0, z], ref[1, z]
    keep = lax.broadcasted_iota(I32, pair.shape, 0) < 4
    keep = jnp.logical_not(keep) if top else keep
    return (
        jnp.where(keep, pair, 0.0),
        jnp.where(keep, pltpu.roll(pair, 4, 0), 0.0),
        jnp.where(keep, speed, 0.0),
    )


def corners_kernel(info_ref, left_ref, right_ref, top_ref, bottom_ref, left_out, right_out):
    nx = left_ref.shape[0]
    nz, ny = top_ref.shape[1], top_ref.shape[3]
    lanes = lax.broadcasted_iota(I32, (8, 128), 1)
    for out, own, begin, source in ((left_out, left_ref, 0, 0), (right_out, right_ref, ny - 128, 124)):
        out[8 : 8 + nx, :] = own[...]
        for ref, top, row in ((top_ref, True, 0), (bottom_ref, False, 8 + nx)):
            acc = jnp.zeros((8, 128), F32)
            for z in range(nz):
                base = GROUP * flipped(z, info_ref[0], nz)
                tiles = [v[:, begin : begin + 128] for v in ghost_rows(ref, z, top)]
                acc = packed(acc, base, tiles, source, lanes)
            out[row : row + 8, :] = acc


def windows_kernel(nt, info_ref, left_ref, right_ref, from_left, from_right, top_ref, bottom_ref, own_ref, *outs):
    nz, ny = top_ref.shape[1], top_ref.shape[3]
    rows = left_ref.shape[0]
    step = 16
    lanes = lax.broadcasted_iota(I32, (step, 128), 1)
    inner = lanes & (GROUP - 1)

    def chunk(k, _):
        at = pl.ds(pl.multiple_of(k * step, step), step)
        parts = (from_left[at, :], left_ref[at, :], right_ref[at, :], from_right[at, :])
        windows = []
        for j in range(3):
            moved = [pltpu.roll(part, (4 * i - 4 * j) % 128, 1) for i, part in enumerate(parts)]
            window = jnp.where(
                inner < 4, moved[0], jnp.where(inner < 8, moved[1], jnp.where(inner < 12, moved[2], moved[3]))
            )
            own_ref[j, at, :] = window
            windows.append(window)
        for side, out in zip(sides_of(nt), outs):
            acc = jnp.zeros((step, 128), F32)
            for e, (field, g) in enumerate(edge_entries()):
                moved = pltpu.roll(windows[field], (GROUP * (e - own_plane(nt, side, g, nz))) % 128, 1)
                moved = moved * CODE_SCALES[field]
                acc = jnp.where((lanes >= GROUP * e) & (lanes < GROUP * (e + 1)), moved, acc)
            out[at, :] = jnp.round(acc).astype(I32).astype(I16)
        return 0

    lax.fori_loop(0, rows // step, chunk, 0, unroll=rows // step)
    for side, out in zip(sides_of(nt), outs):
        for e, (field, g) in enumerate(edge_entries()):
            z = flipped(own_plane(nt, side, g, nz), info_ref[0], nz)
            both = jnp.concatenate(
                [ghost_rows(top_ref, z, True)[field], ghost_rows(bottom_ref, z, False)[field]], axis=0
            )
            both = coded(both, field)
            for t in range(ny // 128):
                row = rows + (e * (ny // 128) + t) * 16
                out[row : row + 16, :] = both[:, t * 128 : (t + 1) * 128]


def sources_kernel(
    nt, info_ref, now_hbm, prev_hbm, speed_hbm, msg_hbm, top_ref, bottom_ref, own_ref, *rest
):
    a_ref, b_ref, c_ref, qa_ref, qb_ref, qc_ref, src, qsrc, load_sems, *node_scratch = rest
    nz, nx, ny = now_hbm.shape
    rows = nx + 2 * OFF
    lots = a_ref.shape[0] // rows
    flip = info_ref[0]

    erows = own_ref.shape[1]
    pltpu.make_async_copy(msg_hbm.at[:, pl.ds(0, 8), :], node_scratch[0], node_scratch[3].at[0]).start()
    loads = []
    for i, (field, ref) in enumerate(((now_hbm, a_ref), (prev_hbm, b_ref), (speed_hbm, c_ref))):
        for p in range(nz):
            copy = pltpu.make_async_copy(
                field.at[flipped(p, flip, nz)],
                ref.at[pl.ds(p * rows + OFF, nx), :],
                load_sems.at[i * nz + p],
            )
            copy.start()
            loads.append(copy)

    zero = jnp.zeros((rows, 128), F32)

    def clear_source(k, _):
        src[pl.ds(pl.multiple_of(k * rows, 8), rows), :] = zero
        return 0

    lax.fori_loop(0, src.shape[0] // rows, clear_source, 0)
    for k in range(qsrc.shape[0] // rows):
        qsrc[k * rows : (k + 1) * rows, :] = zero

    place_nodes = find_nodes(nx, ny, msg_hbm, src, qsrc, *node_scratch)
    edge_zero = jnp.zeros((16, ny), F32)
    for ref in (a_ref, b_ref, c_ref):
        for p in range(lots):
            ref[p * rows : p * rows + 16, :] = edge_zero
            ref[p * rows + OFF + nx : (p + 1) * rows, :] = edge_zero
    if nt == 2:
        for ref in (a_ref, b_ref):
            for t in range(ny // 128):
                ref[(lots - 1) * rows : lots * rows, t * 128 : (t + 1) * 128] = zero
    for p in range(nz):
        z = flipped(p, flip, nz)
        for ref, low, high in zip(
            (a_ref, b_ref, c_ref), ghost_rows(top_ref, z, True), ghost_rows(bottom_ref, z, False)
        ):
            ref[p * rows + 8 : p * rows + 16, :] = low
            ref[p * rows + OFF + nx : p * rows + OFF + nx + 8, :] = high
    for j, ref in enumerate((qa_ref, qb_ref, qc_ref)):
        ref[8 : 8 + erows, 0:128] = own_ref[j]
        ref[0:8, 0:128] = jnp.zeros((8, 128), F32)
        ref[8 + erows :, 0:128] = jnp.zeros((rows - 8 - erows, 128), F32)
        ref[:, 128:256] = zero
    place_nodes()
    for copy in loads:
        copy.wait()


def find_nodes(nx, ny, msg_hbm, src, qsrc, msg_ref, spots_ref, spots, in_sems):
    rows = nx + 2 * OFF
    flat = src.shape[0] // (2 * STEPS)
    senders = msg_hbm.shape[0]

    def first_row(at):
        return ((at >> 3) << 5) + (at & 7)

    def spot(word):
        return pl.ds(word >> 7, STEPS, stride=8)

    def msg_copy(r):
        return pltpu.make_async_copy(msg_hbm.at[:, pl.ds(8 * r, 8), :], msg_ref, in_sems.at[0])

    def spots_copy():
        return pltpu.make_async_copy(spots_ref, spots, in_sems.at[1])

    first_msg = msg_copy(0)
    def find_spots(whole):
        code = msg_ref[:, STEPS, :].astype(I32)
        p = code >> 18
        row = (code >> 9) & 511
        col = (code & 511) - 8
        index = lax.broadcasted_iota(I32, code.shape, 1)
        used = code != 0
        t = jnp.clip(col >> 7, 0, ny // 128 - 1)
        inside = used & (col >= 0) & (col < ny)
        spare = (index & 1) * flat + ((index >> 1) & 7)
        at = jnp.where(inside, t * flat + p * rows + row, spare)
        turn = (col - t * 128 - index) & 127
        clash = jnp.zeros(code.shape, I32)
        for j in range(1, BATCH):
            same = (at == pltpu.roll(at, j, 1)) & ((index & (BATCH - 1)) >= j) & (index < 2 * BATCH)
            clash = clash | jnp.where(same, 1, 0)
        word = (first_row(at) << 7) + turn
        spots_ref[0] = jnp.where(clash > 0, (first_row(spare) << 7) + turn, word)
        spots_ref[1] = word if whole else jnp.where((clash > 0) | (index >= 2 * BATCH), word, -1)
        low = col < 4
        qlane = GROUP * (p & 7) + jnp.where(low, col + 4, col - (ny - 4) + 8)
        spots_ref[2] = (first_row((p >> 3) * rows + row) << 7) + ((qlane - index) & 127)
        begin = jnp.where(jnp.max(clash, axis=1, keepdims=True) > 0, 0, 2 * BATCH)
        counts = msg_ref[:, STEPS + 1, :].astype(I32)
        nears = msg_ref[:, STEPS + 2, :].astype(I32)
        spots_ref[3] = jnp.where(index == 0, counts, jnp.where(index == 1, nears, begin))

    first_msg.wait()
    find_spots(False)
    spots_copy().start()
    lane = lax.broadcasted_iota(I32, (8, 128), 1)

    def share(d, k, turn):
        one = jnp.where(lane == k, msg_ref[d], 0.0)
        return pltpu.roll(one, turn, 1)[0:STEPS]

    def place_batch(d, first):
        words = [spots[0, d, k] for k in range(first, first + BATCH)]
        tile = msg_ref[d]
        values = [
            src[spot(word), :] + pltpu.roll(jnp.where(lane == first + k, tile, 0.0), word & 127, 1)[0:STEPS]
            for k, word in enumerate(words)
        ]
        for word, value in zip(words, values):
            src[spot(word), :] = value

    def place_first(d, _):
        place_batch(d, 0)
        return 0

    def place_second(i, _):
        group = [4 * i + j for j in range(4)]
        most = spots[3, group[0], 0]
        for d in group[1:]:
            most = jnp.maximum(most, spots[3, d, 0])

        @pl.when(most > BATCH)
        def _():
            for d in group:
                place_batch(d, BATCH)

        return 0

    def place_rest(r):
        def sender(d, most):
            count = spots[3, d, 0]

            def one(k, _):
                word = spots[1, d, k]

                @pl.when(word >= 0)
                def _():
                    src[spot(word), :] = src[spot(word), :] + share(d, k, word & 127)

                return 0

            def window(k, _):
                word = spots[2, d, k]
                qsrc[spot(word), :] = qsrc[spot(word), :] + share(d, k, word & 127)
                return 0

            first = 0 if r is not None else spots[3, d, 2]
            done = 0 if r is None else r * SLOTS
            lax.fori_loop(first, jnp.clip(count - done, 0, SLOTS), one, 0)
            lax.fori_loop(0, jnp.clip(spots[3, d, 1] - done, 0, SLOTS), window, 0)
            return jnp.maximum(most, count)

        return lax.fori_loop(0, senders, sender, 0)

    def place_nodes():
        spots_copy().wait()
        lax.fori_loop(0, senders, place_first, 0, unroll=4)
        lax.fori_loop(0, senders // 4, place_second, 0)
        most = place_rest(None)

        def extra(r, _):
            again = msg_copy(r)
            again.start()
            again.wait()
            find_spots(True)
            again = spots_copy()
            again.start()
            again.wait()
            place_rest(r)
            return 0

        lax.fori_loop(1, (most + SLOTS - 1) // SLOTS, extra, 0)

    return place_nodes


def steps_kernel(nt, info_ref, *rest):
    sides = sides_of(nt)
    n_side = len(sides)
    src, qsrc, rest = rest[6], rest[7], rest[8:]
    planes_in, rest = rest[:n_side], rest[n_side:]
    edges_in, rest = rest[:n_side], rest[n_side:]
    out_prev, out_now, a_ref, b_ref, c_ref, qa_ref, qb_ref, qc_ref, store_sems = rest
    nz, nx, ny = out_now.shape
    rows = nx + 2 * OFF
    lots = a_ref.shape[0] // rows
    flat = src.shape[0] // (2 * STEPS)
    erows = nx + 16
    flip = info_ref[0]
    for side, planes, edges in zip(sides, planes_in, edges_in):
        for k, (field, g) in enumerate(z_entries(nz)):
            ref = (a_ref, b_ref, c_ref)[field]
            at = ghost_plane(side, g, nz) * rows
            ref[at + OFF : at + OFF + nx, :] = decoded(planes[k], field)
        strip = edges[0:erows, :].astype(I32).astype(F32)
        lanes = lax.broadcasted_iota(I32, strip.shape, 1)
        for e, (field, g) in enumerate(edge_entries()):
            p = ghost_plane(side, g, nz)
            at = p * rows
            ref = (a_ref, b_ref, c_ref)[field]
            for t in range(ny // 128):
                row = erows + (e * (ny // 128) + t) * 16
                both = decoded(edges[row : row + 16, :], field)
                ref[at + 8 : at + 16, t * 128 : (t + 1) * 128] = both[0:8]
                ref[at + OFF + nx : at + OFF + nx + 8, t * 128 : (t + 1) * 128] = both[8:16]
            qref = (qa_ref, qb_ref, qc_ref)[field]
            lot = p - 8
            moved = pltpu.roll(strip, (GROUP * (lot - e)) % 128, 1) * (1.0 / CODE_SCALES[field])
            inside = (lanes >= GROUP * lot) & (lanes < GROUP * (lot + 1))
            qref[8 : 8 + erows, 128:256] = jnp.where(inside, moved, qref[8 : 8 + erows, 128:256])

    size = 16
    lanes = lax.broadcasted_iota(I32, (size, 128), 1)
    first, last = lanes == 0, lanes == 127

    def source_of(ref, at, s):
        return jnp.concatenate(
            [
                ref[pl.ds(pl.multiple_of((at + 8 * k) * STEPS + 8 * s, 8), 8), :]
                for k in range(size // 8)
            ],
            axis=0,
        )

    def main_step(s, now, prev, qnow, after=None):
        more = STEPS - 1 - s
        begin = OFF - 8 if more else OFF
        chunks = (nx + 16 if more else nx) // size

        def plane(i, _):
            p = i if nt == 2 else (i - more + lots) & (lots - 1)
            base = p * rows
            above = lax.rem(p + 1, lots) * rows
            below = lax.rem(p + lots - 1, lots) * rows
            qtile = pl.ds(pl.multiple_of((p >> 3) * 128, 128), 128)
            group = GROUP * (p & 7)
            to_first = lax.rem(256 - 3 - group, 128)
            to_last = lax.rem(256 + 127 - 12 - group, 128)

            def chunk(k, _):
                r0 = pl.multiple_of(begin + k * size, 8)

                def part(ref, at, t, extra=0):
                    at = pl.ds(pl.multiple_of(at + r0 - extra, 8), size + 2 * extra)
                    return ref[at, t * 128 : (t + 1) * 128]

                q = qnow[pl.ds(r0, size), qtile]
                mids = [part(now, base, t) for t in range(2)]
                ahead = [pltpu.roll(mid, 1, 1) for mid in mids]
                behind = [pltpu.roll(mid, 127, 1) for mid in mids]
                left = [
                    jnp.where(first, pltpu.roll(q, to_first, 1), ahead[0]),
                    jnp.where(first, ahead[0], ahead[1]),
                ]
                right = [
                    jnp.where(last, behind[1], behind[0]),
                    jnp.where(last, pltpu.roll(q, to_last, 1), behind[1]),
                ]
                for t in range(2):
                    wide = part(now, base, t, 8)
                    mid = mids[t]
                    beside = part(now, above, t) + part(now, below, t)
                    beside = beside + (wide[7 : 7 + size] + wide[9 : 9 + size])
                    beside = beside + (left[t] + right[t])
                    source = source_of(src, t * flat + base + r0, s)
                    result = (
                        2.0 * mid
                        - part(prev, base, t)
                        + (0.25 * part(c_ref, base, t)) * (beside - 6.0 * mid + source)
                    )
                    at = pl.ds(pl.multiple_of(base + r0, 8), size)
                    prev[at, t * 128 : (t + 1) * 128] = result
                return 0

            lax.fori_loop(0, chunks, chunk, 0, unroll=chunks)
            if after is not None:
                after(i)
            return 0

        lax.fori_loop(0, nz + n_side * more, plane, 0, unroll=True)

    def q_step(s, now, prev):
        def chunk(k, _):
            r0 = pl.multiple_of(OFF - 8 + k * size, 8)
            wide = now[pl.ds(pl.multiple_of(r0 - 8, 8), size + 16), :]
            mid = wide[8 : 8 + size]
            beside = wide[7 : 7 + size] + wide[9 : 9 + size]
            for shift in (1, 255, GROUP, 256 - GROUP):
                beside = beside + pltpu.roll(mid, shift, 1)
            at = pl.ds(r0, size)
            source = jnp.concatenate(
                [source_of(qsrc, r0, s), source_of(qsrc, rows + r0, s)], axis=1
            )
            prev[at, :] = (
                2.0 * mid
                - prev[at, :]
                + (0.25 * qc_ref[at, :]) * (beside - 6.0 * mid + source)
            )
            return 0

        lax.fori_loop(0, (nx + 16) // size, chunk, 0, unroll=(nx + 16) // size)

    fields, windows = [a_ref, b_ref], [qa_ref, qb_ref]

    def store(ref, out, p, sem):
        return pltpu.make_async_copy(
            ref.at[pl.ds(p * rows + OFF, nx), :], out.at[flipped(p, flip, nz)], sem
        )

    for s in range(STEPS - 1):
        main_step(s, fields[0], fields[1], windows[0])
        q_step(s, windows[0], windows[1])
        fields, windows = fields[::-1], windows[::-1]
    for p in range(nz):
        store(fields[0], out_prev, p, store_sems.at[p]).start()

    def finish(p):
        store(fields[1], out_now, p, store_sems.at[nz + p]).start()

    main_step(STEPS - 1, fields[0], fields[1], windows[0], finish)
    for p in range(nz):
        store(fields[0], out_prev, p, store_sems.at[p]).wait()
        store(fields[1], out_now, p, store_sems.at[nz + p]).wait()


def shifted(value, axis, count, step):
    pairs = [(i, i + step) for i in range(count) if 0 <= i + step < count]
    return lax.ppermute(value, axis, pairs)


def to_depth(values, nt):
    if nt == 2:
        return [lax.ppermute(values[0], "trace", [(0, 1), (1, 0)])]
    return [shifted(values[0], "trace", nt, -1), shifted(values[1], "trace", nt, 1)]


def body(traces, coupling, tap_shift, node_tile, node_cell, field_prev, field_now, speed_sq):
    nt, ngx, ngy = (lax.axis_size(axis) for axis in AXES)
    count = nt * ngx * ngy
    nodes = traces.shape[0]
    nz, nx, ny = field_now.shape
    sides = len(sides_of(nt))
    assert nz + 2 * STEPS == 16 and ny == 256
    shape = jax.ShapeDtypeStruct
    flip = lax.axis_index("trace") if nt == 2 else jnp.int32(0)
    info = jnp.full((1,), flip, I32)
    fields = (field_now, field_prev, speed_sq)

    entries = len(z_entries(nz))
    plane_msgs = call(
        functools.partial(planes_kernel, nt),
        [shape((entries, nx, ny), I16)] * sides,
        [smem_spec()] + [any_spec()] * 3,
        [vmem_spec()] * sides,
        [pltpu.VMEM((sides * entries, nx, ny), F32), pltpu.SemaphoreType.DMA((sides * entries,))],
        bytes_accessed=sides * entries * nx * ny * 6,
    )(info, *fields)
    planes = to_depth(plane_msgs, nt)

    left, right, up, down = call(
        strips_kernel,
        [shape((nx, 128), F32)] * 2 + [shape((2, nz, 8, ny), F32)] * 2,
        [smem_spec()] + [any_spec()] * 3,
        [vmem_spec()] * 4,
        [pltpu.VMEM((3, nz, nx, ny), F32), pltpu.SemaphoreType.DMA((3, nz))],
        bytes_accessed=3 * nz * nx * ny * 4,
    )(info, *fields)
    top = shifted(up, "gx", ngx, 1)
    bottom = shifted(down, "gx", ngx, -1)

    rounds = -(-nodes // SLOTS)
    ints = jnp.stack([tap_shift, node_tile[:, 0], node_cell])
    msg = call(
        functools.partial(amp_kernel, (nt, ngx, ngy, nz, nx, ny)),
        shape((count, 8 * rounds, SLOTS), F32),
        [any_spec(), vmem_spec(), vmem_spec(), any_spec()],
        vmem_spec(),
        [pltpu.VMEM((count, nodes), F32)] * 2
        + [pltpu.VMEM((count, SLOTS), F32)] * 2
        + [
            pltpu.VMEM(traces.shape, BF16),
            pltpu.VMEM((STEPS * RATE, NT), F32),
            pltpu.SemaphoreType.DMA((2,)),
        ],
        bytes_accessed=1 << 20,
        flops=1 << 30,
    )(*in_hbm(traces), coupling, ints, *in_hbm(jnp.asarray(sinc_table())))
    msg, top, bottom = lax.optimization_barrier((msg, top, bottom))
    msg = lax.all_to_all(msg, AXES, split_axis=0, concat_axis=0, tiled=True)

    erows = nx + 16
    left, right = call(
        corners_kernel,
        [shape((erows, 128), F32)] * 2,
        [smem_spec()] + [vmem_spec()] * 4,
        [vmem_spec()] * 2,
        bytes_accessed=1 << 20,
    )(info, left, right, top, bottom)
    from_left = shifted(right, "gy", ngy, 1)
    from_right = shifted(left, "gy", ngy, -1)

    edge_rows = erows + len(edge_entries()) * (ny // 128) * 16
    own, *edge_msgs = call(
        functools.partial(windows_kernel, nt),
        [shape((3, erows, 128), F32)] + [shape((edge_rows, 128), I16)] * sides,
        [smem_spec()] + [vmem_spec()] * 6,
        [vmem_spec()] * (1 + sides),
        bytes_accessed=1 << 20,
    )(info, left, right, from_left, from_right, top, bottom)
    edges = to_depth(edge_msgs, nt)

    rows = nx + 2 * OFF
    lots = nz + STEPS + 1 if nt == 2 else nz + 2 * STEPS
    source_lots = nz + STEPS - 1 if nt == 2 else lots
    state = [pltpu.VMEM((lots * rows, ny), F32)] * 3 + [pltpu.VMEM((rows, 256), F32)] * 3
    sources = [
        pltpu.VMEM((2 * source_lots * rows * STEPS, 128), F32),
        pltpu.VMEM((2 * rows * STEPS, 128), F32),
    ]
    held = call(
        functools.partial(sources_kernel, nt),
        state + sources,
        [smem_spec()] + [any_spec()] * 4 + [vmem_spec()] * 3,
        [vmem_spec()] * 8,
        [
            pltpu.SemaphoreType.DMA((3 * nz,)),
            pltpu.VMEM((count, 8, SLOTS), F32),
            pltpu.VMEM((4, count, SLOTS), I32),
            pltpu.SMEM((4, count, SLOTS), I32),
            pltpu.SemaphoreType.DMA((2,)),
        ],
        bytes_accessed=4 * nz * nx * ny * 4,
        flops=nz * nx * ny * 16,
        limit=SMALL_LIMIT,
    )(info, *in_hbm(*fields, msg), top, bottom, own)
    out_prev, out_now, *_ = call(
        functools.partial(steps_kernel, nt),
        [shape((nz, nx, ny), F32)] * 2 + state,
        [smem_spec()] + [vmem_spec()] * (8 + 2 * sides),
        [any_spec()] * 2 + [vmem_spec()] * 6,
        [pltpu.SemaphoreType.DMA((2 * nz,))],
        bytes_accessed=5 * nz * nx * ny * 4,
        flops=nz * nx * ny * STEPS * 16,
        aliases={1 + i: 2 + i for i in range(6)},
        limit=SMALL_LIMIT,
    )(info, *held, *planes, *edges)
    return out_prev, out_now


def solution(mesh):
    placed = (
        P(AXES, None, None),
        P(AXES, None),
        P(AXES),
        P(AXES, None),
        P(AXES),
        P("trace", "gx", "gy"),
        P("trace", "gx", "gy"),
        P("trace", "gx", "gy"),
    )
    return jax.shard_map(
        body,
        mesh=mesh,
        in_specs=placed,
        out_specs=(P("trace", "gx", "gy"), P("trace", "gx", "gy")),
        check_vma=False,
    )
```

```python
import functools

import jax
import jax.numpy as jnp
import numpy as np
from jax import lax
from jax.experimental import pallas as pl
from jax.experimental.pallas import tpu as pltpu
from jax.sharding import PartitionSpec as P

NT = 256
STEPS = 4
RATE = 64
OFF = 16
GROUP = 16
SLOTS = 128
EARLY = 8
BATCH = 16
AXES = ("trace", "gx", "gy")
F32 = jnp.float32
BF16 = jnp.bfloat16
I32 = jnp.int32
I16 = jnp.int16
CODE_SCALES = (32767.0 / 0.3125, 32767.0 / 0.3125, 32767.0)
VMEM_LIMIT = 52 * 1024 * 1024
SMALL_LIMIT = 8 * 1024 * 1024


def log2(value):
    assert value & (value - 1) == 0
    return value.bit_length() - 1


def sinc_table():
    u = np.arange(NT)[None, :] + np.arange(STEPS * RATE)[:, None] - (NT - RATE // 2)
    u = u.astype(np.float64)
    table = np.sinc(u / RATE) * 0.5 * (1.0 + np.cos(np.pi * u / (2.0 * RATE)))
    return np.where(np.abs(u) < 2.0 * RATE, table, 0.0).astype(np.float32)


def vmem_spec():
    return pl.BlockSpec(memory_space=pltpu.VMEM)


def any_spec():
    return pl.BlockSpec(memory_space=pl.ANY)


def smem_spec():
    return pl.BlockSpec(memory_space=pltpu.SMEM)


def call(
    kernel, outs, in_specs, out_specs, scratch=(), bytes_accessed=0, flops=0, aliases=None,
    limit=VMEM_LIMIT
):
    return pl.pallas_call(
        kernel,
        out_shape=outs,
        in_specs=in_specs,
        out_specs=out_specs,
        scratch_shapes=list(scratch),
        input_output_aliases=aliases or {},
        compiler_params=pltpu.CompilerParams(vmem_limit_bytes=limit),
        cost_estimate=pl.CostEstimate(
            flops=flops, bytes_accessed=bytes_accessed, transcendentals=0
        ),
    )


def coded(values, field):
    return jnp.round(values * CODE_SCALES[field]).astype(I32).astype(I16)


def decoded(codes, field):
    return codes.astype(I32).astype(F32) * (1.0 / CODE_SCALES[field])


def in_hbm(*values):
    return [pltpu.with_memory_space_constraint(value, pltpu.HBM) for value in values]


def split3(values):
    first = values.astype(BF16).astype(F32)
    rest = values - first
    second = rest.astype(BF16).astype(F32)
    third = (rest - second).astype(BF16).astype(F32)
    return first, second, third


def amp_kernel(
    dims, traces_hbm, coupling_ref, ints_ref, table_hbm, out_ref,
    rank_ref, code_ref, count_ref, near_ref, traces_ref, table_ref, sems,
):
    nt, ngx, ngy, nz, nx, ny = dims
    count = nt * ngx * ngy
    nodes = traces_ref.shape[0]
    traces_copy = pltpu.make_async_copy(traces_hbm, traces_ref, sems.at[0])
    table_copy = pltpu.make_async_copy(table_hbm, table_ref, sems.at[1])
    traces_copy.start()
    table_copy.start()
    shift = ints_ref[0:1, :]
    tile = ints_ref[1:2, :]
    cell = ints_ref[2:3, :]
    gz = (tile >> log2(ngx * ngy)) * nz + (cell >> log2(nx * ny))
    gx = ((tile >> log2(ngy)) & (ngx - 1)) * nx + ((cell >> log2(ny)) & (nx - 1))
    gy = (tile & (ngy - 1)) * ny + (cell & (ny - 1))
    dest = lax.broadcasted_iota(I32, (count, nodes), 0)
    da = dest >> log2(ngx * ngy)
    lz = gz - da * nz
    lx = gx - ((dest >> log2(ngy)) & (ngx - 1)) * nx
    ly = gy - (dest & (ngy - 1)) * ny
    far = jnp.zeros((count, nodes), I32)
    for local, size in ((lz, nz), (lx, nx), (ly, ny)):
        far = far + jnp.maximum(-local, 0) + jnp.maximum(local - (size - 1), 0)
    held = far <= STEPS - 1
    plane = lz + da * (nz - 1 - 2 * lz) if nt == 2 else lz & 15
    code_ref[...] = ((plane << 18) + ((lx + OFF) << 9) + (ly + 8)).astype(F32)
    near = held & ((ly < 4) | (ly >= ny - 4))
    held_f = jnp.where(held, 1.0, 0.0)
    near_f = jnp.where(near, 1.0, 0.0)
    before = jnp.where(
        lax.broadcasted_iota(I32, (nodes, nodes), 0) < lax.broadcasted_iota(I32, (nodes, nodes), 1),
        1.0,
        0.0,
    )
    both = jnp.concatenate([held_f, near_f], axis=0).astype(BF16)
    rank = jnp.dot(both, before.astype(BF16), preferred_element_type=F32)
    rank, near_rank = rank[:count], rank[count:]
    counts = jnp.sum(held_f, axis=1, keepdims=True)
    nears = jnp.sum(near_f, axis=1, keepdims=True)
    rank = jnp.where(near, near_rank, nears + rank - near_rank)
    rank_ref[...] = jnp.where(held, rank, -1000.0)
    count_ref[...] = jnp.broadcast_to(counts, count_ref.shape)
    near_ref[...] = jnp.broadcast_to(nears, near_ref.shape)

    slot = lax.broadcasted_iota(I32, (SLOTS, nodes), 0).astype(F32)
    sub = lax.broadcasted_iota(I32, (8, nodes), 0)
    row = lax.broadcasted_iota(I32, (8, SLOTS), 0)
    traces_copy.wait()
    table_copy.wait()
    coupling = coupling_ref[...].astype(F32)
    combined = traces_ref[:, 0, :].astype(F32) * coupling[:, 0:1]
    for c in range(1, traces_ref.shape[1]):
        combined = combined + traces_ref[:, c, :].astype(F32) * coupling[:, c : c + 1]
    every = lax.dot_general(
        table_ref[...],
        combined,
        (((1,), (1,)), ((), ())),
        precision=lax.Precision.HIGHEST,
        preferred_element_type=F32,
    )
    tap = lax.broadcasted_iota(I32, every.shape, 0) & (RATE - 1)
    chosen = jnp.where(tap == shift, every, 0.0)
    amps = jnp.concatenate(
        [
            jnp.sum(chosen[s * RATE : (s + 1) * RATE], axis=0, keepdims=True)
            for s in range(STEPS)
        ],
        axis=0,
    )
    amp_parts = [jnp.concatenate([part, jnp.zeros_like(part)], axis=0) for part in split3(amps)]

    def tile_of(d, offset):
        hit = jnp.where(slot == rank_ref[pl.ds(d, 1), :] - offset, 1.0, 0.0)
        left = [
            jnp.where(sub == STEPS, code, part)
            for part, code in zip(amp_parts, split3(code_ref[pl.ds(d, 1), :]))
        ]
        got = lax.dot_general(
            jnp.concatenate(left, axis=0).astype(BF16),
            hit.astype(BF16),
            (((1,), (1,)), ((), ())),
            preferred_element_type=F32,
        )
        tile = jnp.where(row == STEPS + 1, count_ref[pl.ds(d, 1), :], got[0:8] + got[8:16] + got[16:24])
        return jnp.where(row == STEPS + 2, near_ref[pl.ds(d, 1), :], tile)

    out_ref[:, 8:, :] = jnp.zeros((count, out_ref.shape[1] - 8, SLOTS), F32)

    def first_tile(d, _):
        out_ref[d, 0:8, :] = tile_of(d, 0.0)
        return 0

    lax.fori_loop(0, count, first_tile, 0, unroll=8)

    @pl.when(jnp.max(counts) > SLOTS)
    def _():
        for r in range(1, out_ref.shape[1] // 8):

            def next_tile(d, _):
                out_ref[d, 8 * r : 8 * r + 8, :] = tile_of(d, r * float(SLOTS))
                return 0

            lax.fori_loop(0, count, next_tile, 0, unroll=8)


def z_entries(nz):
    return (
        [(0, g) for g in range(1, STEPS + 1)]
        + [(1, g) for g in range(1, STEPS)]
        + [(2, g) for g in range(1, STEPS)]
    )


def edge_entries():
    return (
        [(0, g) for g in range(1, STEPS)]
        + [(1, g) for g in range(1, STEPS - 1)]
        + [(2, g) for g in range(1, STEPS - 1)]
    )


def sides_of(nt):
    return ("hi",) if nt == 2 else ("hi", "lo")


def own_plane(nt, side, g, nz):
    return nz - g if nt == 2 or side == "lo" else g - 1


def ghost_plane(side, g, nz):
    return nz - 1 + g if side == "hi" else 16 - g


def flipped(plane, flip, nz):
    return plane + flip * (nz - 1 - 2 * plane)


def planes_kernel(nt, info_ref, now_ref, prev_ref, speed_ref, *rest):
    outs, (buffer, sems) = rest[:-2], rest[-2:]
    nz = now_ref.shape[0]
    flip = info_ref[0]
    copies = []
    for i, side in enumerate(sides_of(nt)):
        for k, (field, g) in enumerate(z_entries(nz)):
            source = (now_ref, prev_ref, speed_ref)[field]
            z = flipped(own_plane(nt, side, g, nz), flip, nz)
            at = i * len(z_entries(nz)) + k
            copy = pltpu.make_async_copy(source.at[z], buffer.at[at], sems.at[at])
            copy.start()
            copies.append((copy, i, k, at, field))
    for copy, i, k, at, field in copies:
        copy.wait()
        out, first = (outs[2 * i], 0) if k < EARLY else (outs[2 * i + 1], EARLY)
        out[k - first] = coded(buffer[at], field)


def packed(acc, base, tiles, source, lanes):
    for j, tile in enumerate(tiles):
        start = base + 4 * j
        moved = pltpu.roll(tile, lax.rem(start - source + 128, 128), 1)
        acc = jnp.where((lanes >= start) & (lanes < start + 4), moved, acc)
    return acc


def rows_kernel(now_hbm, prev_hbm, speed_hbm, up_ref, down_ref, buffer, sems):
    nz, nx, ny = now_hbm.shape
    copies = []
    for j, field in enumerate((now_hbm, prev_hbm, speed_hbm)):
        for i, begin in enumerate((nx - 8, 0)):
            copy = pltpu.make_async_copy(
                field.at[:, pl.ds(begin, 8), :], buffer.at[j, i], sems.at[j, i]
            )
            copy.start()
            copies.append(copy)
    for copy in copies:
        copy.wait()
    low = lax.broadcasted_iota(I32, (8, ny), 0) < 4
    for z in range(nz):
        up_ref[0, z] = jnp.where(low, pltpu.roll(buffer[1, 0, z], 4, 0), buffer[0, 0, z])
        up_ref[1, z] = buffer[2, 0, z]
        down_ref[0, z] = jnp.where(low, buffer[0, 1, z], pltpu.roll(buffer[1, 1, z], 4, 0))
        down_ref[1, z] = buffer[2, 1, z]


def ghost_rows(ref, z, top):
    pair, speed = ref[0, z], ref[1, z]
    keep = lax.broadcasted_iota(I32, pair.shape, 0) < 4
    keep = jnp.logical_not(keep) if top else keep
    return (
        jnp.where(keep, pair, 0.0),
        jnp.where(keep, pltpu.roll(pair, 4, 0), 0.0),
        jnp.where(keep, speed, 0.0),
    )


def columns_kernel(
    info_ref, now_hbm, prev_hbm, speed_hbm, top_ref, bottom_ref, left_ref, right_ref, buffer, sems
):
    nz, nx, ny = now_hbm.shape
    flip = info_ref[0]
    copies = []
    for z in range(nz):
        for j, field in enumerate((now_hbm, prev_hbm, speed_hbm)):
            copy = pltpu.make_async_copy(field.at[z], buffer.at[j, z], sems.at[j, z])
            copy.start()
            copies.append(copy)
    sides = ((left_ref, 0, 0), (right_ref, ny - 128, 124))
    lanes = lax.broadcasted_iota(I32, (8, 128), 1)
    for out, begin, source in sides:
        for ref, top, row in ((top_ref, True, 0), (bottom_ref, False, 8 + nx)):
            acc = jnp.zeros((8, 128), F32)
            for z in range(nz):
                base = GROUP * flipped(z, flip, nz)
                tiles = [v[:, begin : begin + 128] for v in ghost_rows(ref, z, top)]
                acc = packed(acc, base, tiles, source, lanes)
            out[row : row + 8, :] = acc
        out[8 : 8 + nx, :] = jnp.zeros((nx, 128), F32)
    rows = 64
    lanes = lax.broadcasted_iota(I32, (rows, 128), 1)
    for z in range(nz):
        for copy in copies[3 * z : 3 * z + 3]:
            copy.wait()
        base = GROUP * flipped(z, flip, nz)
        for k in range(nx // rows):
            at = slice(k * rows, (k + 1) * rows)
            to = slice(8 + k * rows, 8 + (k + 1) * rows)
            for ref, begin, source in sides:
                tiles = [buffer[j, z, at, begin : begin + 128] for j in range(3)]
                ref[to, :] = packed(ref[to, :], base, tiles, source, lanes)


def windows_kernel(nt, info_ref, left_ref, right_ref, from_left, from_right, top_ref, bottom_ref, own_ref, *outs):
    nz, ny = top_ref.shape[1], top_ref.shape[3]
    rows = left_ref.shape[0]
    step = 16
    lanes = lax.broadcasted_iota(I32, (step, 128), 1)
    inner = lanes & (GROUP - 1)

    def chunk(k, _):
        at = pl.ds(pl.multiple_of(k * step, step), step)
        parts = (from_left[at, :], left_ref[at, :], right_ref[at, :], from_right[at, :])
        windows = []
        for j in range(3):
            moved = [pltpu.roll(part, (4 * i - 4 * j) % 128, 1) for i, part in enumerate(parts)]
            window = jnp.where(
                inner < 4, moved[0], jnp.where(inner < 8, moved[1], jnp.where(inner < 12, moved[2], moved[3]))
            )
            own_ref[j, at, :] = window
            windows.append(window)
        for side, out in zip(sides_of(nt), outs):
            acc = jnp.zeros((step, 128), F32)
            for e, (field, g) in enumerate(edge_entries()):
                moved = pltpu.roll(windows[field], (GROUP * (e - own_plane(nt, side, g, nz))) % 128, 1)
                moved = moved * CODE_SCALES[field]
                acc = jnp.where((lanes >= GROUP * e) & (lanes < GROUP * (e + 1)), moved, acc)
            out[at, :] = jnp.round(acc).astype(I32).astype(I16)
        return 0

    lax.fori_loop(0, rows // step, chunk, 0, unroll=rows // step)
    for side, out in zip(sides_of(nt), outs):
        for e, (field, g) in enumerate(edge_entries()):
            z = flipped(own_plane(nt, side, g, nz), info_ref[0], nz)
            both = jnp.concatenate(
                [ghost_rows(top_ref, z, True)[field], ghost_rows(bottom_ref, z, False)[field]], axis=0
            )
            both = coded(both, field)
            for t in range(ny // 128):
                row = rows + (e * (ny // 128) + t) * 16
                out[row : row + 16, :] = both[:, t * 128 : (t + 1) * 128]


def sources_kernel(
    nt, info_ref, now_hbm, prev_hbm, speed_hbm, msg_hbm, top_ref, bottom_ref, own_ref, *rest
):
    a_ref, b_ref, c_ref, qa_ref, qb_ref, qc_ref, src, qsrc, load_sems, *node_scratch = rest
    nz, nx, ny = now_hbm.shape
    rows = nx + 2 * OFF
    lots = a_ref.shape[0] // rows
    flip = info_ref[0]

    erows = own_ref.shape[1]
    pltpu.make_async_copy(msg_hbm.at[:, pl.ds(0, 8), :], node_scratch[0], node_scratch[3].at[0]).start()
    loads = []
    for i, (field, ref) in enumerate(((now_hbm, a_ref), (prev_hbm, b_ref), (speed_hbm, c_ref))):
        for p in range(nz):
            copy = pltpu.make_async_copy(
                field.at[flipped(p, flip, nz)],
                ref.at[pl.ds(p * rows + OFF, nx), :],
                load_sems.at[i * nz + p],
            )
            copy.start()
            loads.append(copy)

    zero = jnp.zeros((rows, 128), F32)
    edge_zero = jnp.zeros((16, ny), F32)
    for ref in (a_ref, b_ref, c_ref):
        for p in range(lots):
            ref[p * rows : p * rows + 16, :] = edge_zero
            ref[p * rows + OFF + nx : (p + 1) * rows, :] = edge_zero
    if nt == 2:
        for ref in (a_ref, b_ref):
            for t in range(ny // 128):
                ref[(lots - 1) * rows : lots * rows, t * 128 : (t + 1) * 128] = zero
    for p in range(nz):
        z = flipped(p, flip, nz)
        for ref, low, high in zip(
            (a_ref, b_ref, c_ref), ghost_rows(top_ref, z, True), ghost_rows(bottom_ref, z, False)
        ):
            ref[p * rows + 8 : p * rows + 16, :] = low
            ref[p * rows + OFF + nx : p * rows + OFF + nx + 8, :] = high
    for j, ref in enumerate((qa_ref, qb_ref, qc_ref)):
        ref[8 : 8 + erows, 0:128] = own_ref[j]
        ref[0:8, 0:128] = jnp.zeros((8, 128), F32)
        ref[8 + erows :, 0:128] = jnp.zeros((rows - 8 - erows, 128), F32)
        ref[:, 128:256] = zero
    place_nodes = find_nodes(nx, ny, msg_hbm, src, qsrc, *node_scratch)

    def clear_source(k, _):
        src[pl.ds(pl.multiple_of(k * rows, 8), rows), :] = zero
        return 0

    lax.fori_loop(0, src.shape[0] // rows, clear_source, 0)
    for k in range(qsrc.shape[0] // rows):
        qsrc[k * rows : (k + 1) * rows, :] = zero
    place_nodes()
    for copy in loads:
        copy.wait()


def find_nodes(nx, ny, msg_hbm, src, qsrc, msg_ref, spots_ref, spots, in_sems):
    rows = nx + 2 * OFF
    flat = src.shape[0] // (2 * STEPS)
    senders = msg_hbm.shape[0]

    def first_row(at):
        return ((at >> 3) << 5) + (at & 7)

    def spot(word):
        return pl.ds(word >> 7, STEPS, stride=8)

    def msg_copy(r):
        return pltpu.make_async_copy(msg_hbm.at[:, pl.ds(8 * r, 8), :], msg_ref, in_sems.at[0])

    def spots_copy():
        return pltpu.make_async_copy(spots_ref, spots, in_sems.at[1])

    first_msg = msg_copy(0)
    def find_spots(whole):
        code = msg_ref[:, STEPS, :].astype(I32)
        p = code >> 18
        row = (code >> 9) & 511
        col = (code & 511) - 8
        index = lax.broadcasted_iota(I32, code.shape, 1)
        used = code != 0
        t = jnp.clip(col >> 7, 0, ny // 128 - 1)
        inside = used & (col >= 0) & (col < ny)
        spare = (index & 1) * flat + ((index >> 1) & 7)
        at = jnp.where(inside, t * flat + p * rows + row, spare)
        turn = (col - t * 128 - index) & 127
        clash = jnp.zeros(code.shape, I32)
        for j in range(1, BATCH):
            same = (at == pltpu.roll(at, j, 1)) & ((index & (BATCH - 1)) >= j) & (index < 2 * BATCH)
            clash = clash | jnp.where(same, 1, 0)
        word = (first_row(at) << 7) + turn
        spots_ref[0] = jnp.where(clash > 0, (first_row(spare) << 7) + turn, word)
        spots_ref[1] = word if whole else jnp.where((clash > 0) | (index >= 2 * BATCH), word, -1)
        low = col < 4
        qlane = GROUP * (p & 7) + jnp.where(low, col + 4, col - (ny - 4) + 8)
        spots_ref[2] = (first_row((p >> 3) * rows + row) << 7) + ((qlane - index) & 127)
        begin = jnp.where(jnp.max(clash, axis=1, keepdims=True) > 0, 0, 2 * BATCH)
        counts = msg_ref[:, STEPS + 1, :].astype(I32)
        nears = msg_ref[:, STEPS + 2, :].astype(I32)
        spots_ref[3] = jnp.where(index == 0, counts, jnp.where(index == 1, nears, begin))

    first_msg.wait()
    find_spots(False)
    spots_copy().start()
    lane = lax.broadcasted_iota(I32, (8, 128), 1)

    def share(d, k, turn):
        one = jnp.where(lane == k, msg_ref[d], 0.0)
        return pltpu.roll(one, turn, 1)[0:STEPS]

    def place_batch(d, first):
        words = [spots[0, d, k] for k in range(first, first + BATCH)]
        tile = msg_ref[d]
        values = [
            src[spot(word), :] + pltpu.roll(jnp.where(lane == first + k, tile, 0.0), word & 127, 1)[0:STEPS]
            for k, word in enumerate(words)
        ]
        for word, value in zip(words, values):
            src[spot(word), :] = value

    def place_first(d, _):
        place_batch(d, 0)
        return 0

    def place_second(i, _):
        group = [4 * i + j for j in range(4)]
        most = spots[3, group[0], 0]
        for d in group[1:]:
            most = jnp.maximum(most, spots[3, d, 0])

        @pl.when(most > BATCH)
        def _():
            for d in group:
                place_batch(d, BATCH)

        return 0

    def place_rest(r):
        def sender(d, most):
            count = spots[3, d, 0]

            def one(k, _):
                word = spots[1, d, k]

                @pl.when(word >= 0)
                def _():
                    src[spot(word), :] = src[spot(word), :] + share(d, k, word & 127)

                return 0

            def window(k, _):
                word = spots[2, d, k]
                qsrc[spot(word), :] = qsrc[spot(word), :] + share(d, k, word & 127)
                return 0

            first = 0 if r is not None else spots[3, d, 2]
            done = 0 if r is None else r * SLOTS
            lax.fori_loop(first, jnp.clip(count - done, 0, SLOTS), one, 0)
            lax.fori_loop(0, jnp.clip(spots[3, d, 1] - done, 0, SLOTS), window, 0)
            return jnp.maximum(most, count)

        return lax.fori_loop(0, senders, sender, 0)

    def place_nodes():
        spots_copy().wait()
        lax.fori_loop(0, senders, place_first, 0, unroll=4)
        lax.fori_loop(0, senders // 4, place_second, 0)
        most = place_rest(None)

        def extra(r, _):
            again = msg_copy(r)
            again.start()
            again.wait()
            find_spots(True)
            again = spots_copy()
            again.start()
            again.wait()
            place_rest(r)
            return 0

        lax.fori_loop(1, (most + SLOTS - 1) // SLOTS, extra, 0)

    return place_nodes


def steps_kernel(nt, info_ref, *rest):
    sides = sides_of(nt)
    n_side = len(sides)
    src, qsrc, rest = rest[6], rest[7], rest[8:]
    planes_in, rest = rest[:n_side], rest[n_side:]
    later_in, rest = rest[:n_side], rest[n_side:]
    edges_in, rest = rest[:n_side], rest[n_side:]
    out_prev, out_now, a_ref, b_ref, c_ref, qa_ref, qb_ref, qc_ref, store_sems = rest
    nz, nx, ny = out_now.shape
    rows = nx + 2 * OFF
    lots = a_ref.shape[0] // rows
    flat = src.shape[0] // (2 * STEPS)
    erows = nx + 16
    flip = info_ref[0]
    for side, planes, later, edges in zip(sides, planes_in, later_in, edges_in):
        for k, (field, g) in enumerate(z_entries(nz)):
            ref = (a_ref, b_ref, c_ref)[field]
            at = ghost_plane(side, g, nz) * rows
            ref[at + OFF : at + OFF + nx, :] = decoded(planes[k] if k < EARLY else later[k - EARLY], field)
        strip = edges[0:erows, :].astype(I32).astype(F32)
        lanes = lax.broadcasted_iota(I32, strip.shape, 1)
        for e, (field, g) in enumerate(edge_entries()):
            p = ghost_plane(side, g, nz)
            at = p * rows
            ref = (a_ref, b_ref, c_ref)[field]
            for t in range(ny // 128):
                row = erows + (e * (ny // 128) + t) * 16
                both = decoded(edges[row : row + 16, :], field)
                ref[at + 8 : at + 16, t * 128 : (t + 1) * 128] = both[0:8]
                ref[at + OFF + nx : at + OFF + nx + 8, t * 128 : (t + 1) * 128] = both[8:16]
            qref = (qa_ref, qb_ref, qc_ref)[field]
            lot = p - 8
            moved = pltpu.roll(strip, (GROUP * (lot - e)) % 128, 1) * (1.0 / CODE_SCALES[field])
            inside = (lanes >= GROUP * lot) & (lanes < GROUP * (lot + 1))
            qref[8 : 8 + erows, 128:256] = jnp.where(inside, moved, qref[8 : 8 + erows, 128:256])

    size = 16
    lanes = lax.broadcasted_iota(I32, (size, 128), 1)
    first, last = lanes == 0, lanes == 127

    def source_of(ref, at, s):
        return jnp.concatenate(
            [
                ref[pl.ds(pl.multiple_of((at + 8 * k) * STEPS + 8 * s, 8), 8), :]
                for k in range(size // 8)
            ],
            axis=0,
        )

    def main_step(s, now, prev, qnow, after=None):
        more = STEPS - 1 - s
        begin = OFF - 8 if more else OFF
        chunks = (nx + 16 if more else nx) // size

        def plane(i, _):
            p = i if nt == 2 else (i - more + lots) & (lots - 1)
            base = p * rows
            above = lax.rem(p + 1, lots) * rows
            below = lax.rem(p + lots - 1, lots) * rows
            qtile = pl.ds(pl.multiple_of((p >> 3) * 128, 128), 128)
            group = GROUP * (p & 7)
            to_first = lax.rem(256 - 3 - group, 128)
            to_last = lax.rem(256 + 127 - 12 - group, 128)

            def chunk(k, _):
                r0 = pl.multiple_of(begin + k * size, 8)

                def part(ref, at, t, extra=0):
                    at = pl.ds(pl.multiple_of(at + r0 - extra, 8), size + 2 * extra)
                    return ref[at, t * 128 : (t + 1) * 128]

                q = qnow[pl.ds(r0, size), qtile]
                mids = [part(now, base, t) for t in range(2)]
                ahead = [pltpu.roll(mid, 1, 1) for mid in mids]
                behind = [pltpu.roll(mid, 127, 1) for mid in mids]
                left = [
                    jnp.where(first, pltpu.roll(q, to_first, 1), ahead[0]),
                    jnp.where(first, ahead[0], ahead[1]),
                ]
                right = [
                    jnp.where(last, behind[1], behind[0]),
                    jnp.where(last, pltpu.roll(q, to_last, 1), behind[1]),
                ]
                for t in range(2):
                    wide = part(now, base, t, 8)
                    mid = mids[t]
                    beside = part(now, above, t) + part(now, below, t)
                    beside = beside + (wide[7 : 7 + size] + wide[9 : 9 + size])
                    beside = beside + (left[t] + right[t])
                    source = source_of(src, t * flat + base + r0, s)
                    result = (
                        2.0 * mid
                        - part(prev, base, t)
                        + (0.25 * part(c_ref, base, t)) * (beside - 6.0 * mid + source)
                    )
                    at = pl.ds(pl.multiple_of(base + r0, 8), size)
                    prev[at, t * 128 : (t + 1) * 128] = result
                return 0

            lax.fori_loop(0, chunks, chunk, 0, unroll=chunks)
            if after is not None:
                after(i)
            return 0

        lax.fori_loop(0, nz + n_side * more, plane, 0, unroll=True)

    def q_step(s, now, prev):
        def chunk(k, _):
            r0 = pl.multiple_of(OFF - 8 + k * size, 8)
            wide = now[pl.ds(pl.multiple_of(r0 - 8, 8), size + 16), :]
            mid = wide[8 : 8 + size]
            beside = wide[7 : 7 + size] + wide[9 : 9 + size]
            for shift in (1, 255, GROUP, 256 - GROUP):
                beside = beside + pltpu.roll(mid, shift, 1)
            at = pl.ds(r0, size)
            source = jnp.concatenate(
                [source_of(qsrc, r0, s), source_of(qsrc, rows + r0, s)], axis=1
            )
            prev[at, :] = (
                2.0 * mid
                - prev[at, :]
                + (0.25 * qc_ref[at, :]) * (beside - 6.0 * mid + source)
            )
            return 0

        lax.fori_loop(0, (nx + 16) // size, chunk, 0, unroll=(nx + 16) // size)

    fields, windows = [a_ref, b_ref], [qa_ref, qb_ref]

    def store(ref, out, p, sem):
        return pltpu.make_async_copy(
            ref.at[pl.ds(p * rows + OFF, nx), :], out.at[flipped(p, flip, nz)], sem
        )

    for s in range(STEPS - 1):
        main_step(s, fields[0], fields[1], windows[0])
        q_step(s, windows[0], windows[1])
        fields, windows = fields[::-1], windows[::-1]
    for p in range(nz):
        store(fields[0], out_prev, p, store_sems.at[p]).start()

    def finish(p):
        store(fields[1], out_now, p, store_sems.at[nz + p]).start()

    main_step(STEPS - 1, fields[0], fields[1], windows[0], finish)
    for p in range(nz):
        store(fields[0], out_prev, p, store_sems.at[p]).wait()
        store(fields[1], out_now, p, store_sems.at[nz + p]).wait()


def shifted(value, axis, count, step):
    pairs = [(i, i + step) for i in range(count) if 0 <= i + step < count]
    return lax.ppermute(value, axis, pairs)


def to_depth(values, nt):
    if nt == 2:
        return [lax.ppermute(values[0], "trace", [(0, 1), (1, 0)])]
    return [shifted(values[0], "trace", nt, -1), shifted(values[1], "trace", nt, 1)]


def body(traces, coupling, tap_shift, node_tile, node_cell, field_prev, field_now, speed_sq):
    nt, ngx, ngy = (lax.axis_size(axis) for axis in AXES)
    count = nt * ngx * ngy
    nodes = traces.shape[0]
    nz, nx, ny = field_now.shape
    sides = len(sides_of(nt))
    assert nz + 2 * STEPS == 16 and ny == 256
    shape = jax.ShapeDtypeStruct
    flip = lax.axis_index("trace") if nt == 2 else jnp.int32(0)
    info = jnp.full((1,), flip, I32)
    fields = (field_now, field_prev, speed_sq)

    entries = len(z_entries(nz))
    plane_msgs = call(
        functools.partial(planes_kernel, nt),
        [shape((EARLY, nx, ny), I16), shape((entries - EARLY, nx, ny), I16)] * sides,
        [smem_spec()] + [any_spec()] * 3,
        [vmem_spec()] * (2 * sides),
        [pltpu.VMEM((sides * entries, nx, ny), F32), pltpu.SemaphoreType.DMA((sides * entries,))],
        bytes_accessed=sides * entries * nx * ny * 6,
    )(info, *fields)
    planes = to_depth(plane_msgs[0::2], nt)

    up, down = call(
        rows_kernel,
        [shape((2, nz, 8, ny), F32)] * 2,
        [any_spec()] * 3,
        [vmem_spec()] * 2,
        [pltpu.VMEM((3, 2, nz, 8, ny), F32), pltpu.SemaphoreType.DMA((3, 2))],
        bytes_accessed=1 << 20,
    )(*fields)
    top = shifted(up, "gx", ngx, 1)
    bottom = shifted(down, "gx", ngx, -1)

    rounds = -(-nodes // SLOTS)
    ints = jnp.stack([tap_shift, node_tile[:, 0], node_cell])
    msg = call(
        functools.partial(amp_kernel, (nt, ngx, ngy, nz, nx, ny)),
        shape((count, 8 * rounds, SLOTS), F32),
        [any_spec(), vmem_spec(), vmem_spec(), any_spec()],
        vmem_spec(),
        [pltpu.VMEM((count, nodes), F32)] * 2
        + [pltpu.VMEM((count, SLOTS), F32)] * 2
        + [
            pltpu.VMEM(traces.shape, BF16),
            pltpu.VMEM((STEPS * RATE, NT), F32),
            pltpu.SemaphoreType.DMA((2,)),
        ],
        bytes_accessed=1 << 20,
        flops=1 << 30,
    )(*in_hbm(traces), coupling, ints, *in_hbm(jnp.asarray(sinc_table())))
    msg, top, bottom = lax.optimization_barrier((msg, top, bottom))
    msg = lax.all_to_all(msg, AXES, split_axis=0, concat_axis=0, tiled=True)

    erows = nx + 16
    left, right = call(
        columns_kernel,
        [shape((erows, 128), F32)] * 2,
        [smem_spec()] + [any_spec()] * 3 + [vmem_spec()] * 2,
        [vmem_spec()] * 2,
        [pltpu.VMEM((3, nz, nx, ny), F32), pltpu.SemaphoreType.DMA((3, nz))],
        bytes_accessed=3 * nz * nx * ny * 4,
    )(info, *fields, top, bottom)
    from_left = shifted(right, "gy", ngy, 1)
    from_right = shifted(left, "gy", ngy, -1)
    from_left, from_right, *later = lax.optimization_barrier(
        (from_left, from_right, *plane_msgs[1::2])
    )
    later = to_depth(later, nt)

    edge_rows = erows + len(edge_entries()) * (ny // 128) * 16
    own, *edge_msgs = call(
        functools.partial(windows_kernel, nt),
        [shape((3, erows, 128), F32)] + [shape((edge_rows, 128), I16)] * sides,
        [smem_spec()] + [vmem_spec()] * 6,
        [vmem_spec()] * (1 + sides),
        bytes_accessed=1 << 20,
    )(info, left, right, from_left, from_right, top, bottom)
    edges = to_depth(edge_msgs, nt)

    rows = nx + 2 * OFF
    lots = nz + STEPS + 1 if nt == 2 else nz + 2 * STEPS
    source_lots = nz + STEPS - 1 if nt == 2 else lots
    state = [pltpu.VMEM((lots * rows, ny), F32)] * 3 + [pltpu.VMEM((rows, 256), F32)] * 3
    sources = [
        pltpu.VMEM((2 * source_lots * rows * STEPS, 128), F32),
        pltpu.VMEM((2 * rows * STEPS, 128), F32),
    ]
    held = call(
        functools.partial(sources_kernel, nt),
        state + sources,
        [smem_spec()] + [any_spec()] * 4 + [vmem_spec()] * 3,
        [vmem_spec()] * 8,
        [
            pltpu.SemaphoreType.DMA((3 * nz,)),
            pltpu.VMEM((count, 8, SLOTS), F32),
            pltpu.VMEM((4, count, SLOTS), I32),
            pltpu.SMEM((4, count, SLOTS), I32),
            pltpu.SemaphoreType.DMA((2,)),
        ],
        bytes_accessed=4 * nz * nx * ny * 4,
        flops=nz * nx * ny * 16,
        limit=SMALL_LIMIT,
    )(info, *in_hbm(*fields, msg), top, bottom, own)
    out_prev, out_now, *_ = call(
        functools.partial(steps_kernel, nt),
        [shape((nz, nx, ny), F32)] * 2 + state,
        [smem_spec()] + [vmem_spec()] * (8 + 3 * sides),
        [any_spec()] * 2 + [vmem_spec()] * 6,
        [pltpu.SemaphoreType.DMA((2 * nz,))],
        bytes_accessed=5 * nz * nx * ny * 4,
        flops=nz * nx * ny * STEPS * 16,
        aliases={1 + i: 2 + i for i in range(6)},
        limit=SMALL_LIMIT,
    )(info, *held, *planes, *later, *edges)
    return out_prev, out_now


def solution(mesh):
    placed = (
        P(AXES, None, None),
        P(AXES, None),
        P(AXES),
        P(AXES, None),
        P(AXES),
        P("trace", "gx", "gy"),
        P("trace", "gx", "gy"),
        P("trace", "gx", "gy"),
    )
    return jax.shard_map(
        body,
        mesh=mesh,
        in_specs=placed,
        out_specs=(P("trace", "gx", "gy"), P("trace", "gx", "gy")),
        check_vma=False,
    )
```

```python
import functools

import jax
import jax.numpy as jnp
import numpy as np
from jax import lax
from jax.experimental import pallas as pl
from jax.experimental.pallas import tpu as pltpu
from jax.sharding import PartitionSpec as P

NT = 256
STEPS = 4
RATE = 64
OFF = 16
GROUP = 16
SLOTS = 128
EARLY = 8
BATCH = 16
AXES = ("trace", "gx", "gy")
F32 = jnp.float32
BF16 = jnp.bfloat16
I32 = jnp.int32
I16 = jnp.int16
CODE_SCALES = (32767.0 / 0.3125, 32767.0 / 0.3125, 32767.0)
VMEM_LIMIT = 52 * 1024 * 1024
SMALL_LIMIT = 8 * 1024 * 1024


def log2(value):
    assert value & (value - 1) == 0
    return value.bit_length() - 1


def sinc_table():
    u = np.arange(NT)[None, :] + np.arange(STEPS * RATE)[:, None] - (NT - RATE // 2)
    u = u.astype(np.float64)
    table = np.sinc(u / RATE) * 0.5 * (1.0 + np.cos(np.pi * u / (2.0 * RATE)))
    return np.where(np.abs(u) < 2.0 * RATE, table, 0.0).astype(np.float32)


def vmem_spec():
    return pl.BlockSpec(memory_space=pltpu.VMEM)


def any_spec():
    return pl.BlockSpec(memory_space=pl.ANY)


def smem_spec():
    return pl.BlockSpec(memory_space=pltpu.SMEM)


def call(
    kernel, outs, in_specs, out_specs, scratch=(), bytes_accessed=0, flops=0, aliases=None,
    limit=VMEM_LIMIT
):
    return pl.pallas_call(
        kernel,
        out_shape=outs,
        in_specs=in_specs,
        out_specs=out_specs,
        scratch_shapes=list(scratch),
        input_output_aliases=aliases or {},
        compiler_params=pltpu.CompilerParams(vmem_limit_bytes=limit),
        cost_estimate=pl.CostEstimate(
            flops=flops, bytes_accessed=bytes_accessed, transcendentals=0
        ),
    )


def coded(values, field):
    return jnp.round(values * CODE_SCALES[field]).astype(I32).astype(I16)


def decoded(codes, field):
    return codes.astype(I32).astype(F32) * (1.0 / CODE_SCALES[field])


def in_hbm(*values):
    return [pltpu.with_memory_space_constraint(value, pltpu.HBM) for value in values]


def split3(values):
    first = values.astype(BF16).astype(F32)
    rest = values - first
    second = rest.astype(BF16).astype(F32)
    third = (rest - second).astype(BF16).astype(F32)
    return first, second, third


def amp_kernel(
    dims, traces_hbm, coupling_ref, ints_ref, table_hbm, out_ref,
    rank_ref, code_ref, count_ref, near_ref, traces_ref, table_ref, sems,
):
    nt, ngx, ngy, nz, nx, ny = dims
    count = nt * ngx * ngy
    nodes = traces_ref.shape[0]
    traces_copy = pltpu.make_async_copy(traces_hbm, traces_ref, sems.at[0])
    table_copy = pltpu.make_async_copy(table_hbm, table_ref, sems.at[1])
    traces_copy.start()
    table_copy.start()
    shift = ints_ref[0:1, :]
    tile = ints_ref[1:2, :]
    cell = ints_ref[2:3, :]
    gz = (tile >> log2(ngx * ngy)) * nz + (cell >> log2(nx * ny))
    gx = ((tile >> log2(ngy)) & (ngx - 1)) * nx + ((cell >> log2(ny)) & (nx - 1))
    gy = (tile & (ngy - 1)) * ny + (cell & (ny - 1))
    dest = lax.broadcasted_iota(I32, (count, nodes), 0)
    da = dest >> log2(ngx * ngy)
    lz = gz - da * nz
    lx = gx - ((dest >> log2(ngy)) & (ngx - 1)) * nx
    ly = gy - (dest & (ngy - 1)) * ny
    far = jnp.zeros((count, nodes), I32)
    for local, size in ((lz, nz), (lx, nx), (ly, ny)):
        far = far + jnp.maximum(-local, 0) + jnp.maximum(local - (size - 1), 0)
    held = far <= STEPS - 1
    plane = lz + da * (nz - 1 - 2 * lz) if nt == 2 else lz & 15
    code_ref[...] = ((plane << 18) + ((lx + OFF) << 9) + (ly + 8)).astype(F32)
    near = held & ((ly < 4) | (ly >= ny - 4))
    held_f = jnp.where(held, 1.0, 0.0)
    near_f = jnp.where(near, 1.0, 0.0)
    before = jnp.where(
        lax.broadcasted_iota(I32, (nodes, nodes), 0) < lax.broadcasted_iota(I32, (nodes, nodes), 1),
        1.0,
        0.0,
    )
    both = jnp.concatenate([held_f, near_f], axis=0).astype(BF16)
    rank = jnp.dot(both, before.astype(BF16), preferred_element_type=F32)
    rank, near_rank = rank[:count], rank[count:]
    counts = jnp.sum(held_f, axis=1, keepdims=True)
    nears = jnp.sum(near_f, axis=1, keepdims=True)
    rank = jnp.where(near, near_rank, nears + rank - near_rank)
    rank_ref[...] = jnp.where(held, rank, -1000.0)
    count_ref[...] = jnp.broadcast_to(counts, count_ref.shape)
    near_ref[...] = jnp.broadcast_to(nears, near_ref.shape)

    slot = lax.broadcasted_iota(I32, (SLOTS, nodes), 0).astype(F32)
    sub = lax.broadcasted_iota(I32, (8, nodes), 0)
    row = lax.broadcasted_iota(I32, (8, SLOTS), 0)
    traces_copy.wait()
    table_copy.wait()
    coupling = coupling_ref[...].astype(F32)
    combined = traces_ref[:, 0, :].astype(F32) * coupling[:, 0:1]
    for c in range(1, traces_ref.shape[1]):
        combined = combined + traces_ref[:, c, :].astype(F32) * coupling[:, c : c + 1]
    every = lax.dot_general(
        table_ref[...],
        combined,
        (((1,), (1,)), ((), ())),
        precision=lax.Precision.HIGHEST,
        preferred_element_type=F32,
    )
    tap = lax.broadcasted_iota(I32, every.shape, 0) & (RATE - 1)
    chosen = jnp.where(tap == shift, every, 0.0)
    amps = jnp.concatenate(
        [
            jnp.sum(chosen[s * RATE : (s + 1) * RATE], axis=0, keepdims=True)
            for s in range(STEPS)
        ],
        axis=0,
    )
    amp_parts = [jnp.concatenate([part, jnp.zeros_like(part)], axis=0) for part in split3(amps)]

    def tile_of(d, offset):
        hit = jnp.where(slot == rank_ref[pl.ds(d, 1), :] - offset, 1.0, 0.0)
        left = [
            jnp.where(sub == STEPS, code, part)
            for part, code in zip(amp_parts, split3(code_ref[pl.ds(d, 1), :]))
        ]
        got = lax.dot_general(
            jnp.concatenate(left, axis=0).astype(BF16),
            hit.astype(BF16),
            (((1,), (1,)), ((), ())),
            preferred_element_type=F32,
        )
        tile = jnp.where(row == STEPS + 1, count_ref[pl.ds(d, 1), :], got[0:8] + got[8:16] + got[16:24])
        return jnp.where(row == STEPS + 2, near_ref[pl.ds(d, 1), :], tile)

    out_ref[:, 8:, :] = jnp.zeros((count, out_ref.shape[1] - 8, SLOTS), F32)

    def first_tile(d, _):
        out_ref[d, 0:8, :] = tile_of(d, 0.0)
        return 0

    lax.fori_loop(0, count, first_tile, 0, unroll=8)

    @pl.when(jnp.max(counts) > SLOTS)
    def _():
        for r in range(1, out_ref.shape[1] // 8):

            def next_tile(d, _):
                out_ref[d, 8 * r : 8 * r + 8, :] = tile_of(d, r * float(SLOTS))
                return 0

            lax.fori_loop(0, count, next_tile, 0, unroll=8)


def z_entries(nz):
    return (
        [(0, g) for g in range(1, STEPS + 1)]
        + [(1, g) for g in range(1, STEPS)]
        + [(2, g) for g in range(1, STEPS)]
    )


def edge_entries():
    return (
        [(0, g) for g in range(1, STEPS)]
        + [(1, g) for g in range(1, STEPS - 1)]
        + [(2, g) for g in range(1, STEPS - 1)]
    )


def sides_of(nt):
    return ("hi",) if nt == 2 else ("hi", "lo")


def own_plane(nt, side, g, nz):
    return nz - g if nt == 2 or side == "lo" else g - 1


def ghost_plane(side, g, nz):
    return nz - 1 + g if side == "hi" else 16 - g


def flipped(plane, flip, nz):
    return plane + flip * (nz - 1 - 2 * plane)


def planes_kernel(nt, info_ref, now_ref, prev_ref, speed_ref, *rest):
    outs, (buffer, sems) = rest[:-2], rest[-2:]
    nz = now_ref.shape[0]
    flip = info_ref[0]
    copies = []
    for i, side in enumerate(sides_of(nt)):
        for k, (field, g) in enumerate(z_entries(nz)):
            source = (now_ref, prev_ref, speed_ref)[field]
            z = flipped(own_plane(nt, side, g, nz), flip, nz)
            at = i * len(z_entries(nz)) + k
            copy = pltpu.make_async_copy(source.at[z], buffer.at[at], sems.at[at])
            copy.start()
            copies.append((copy, i, k, at, field))
    for copy, i, k, at, field in copies:
        copy.wait()
        out, first = (outs[2 * i], 0) if k < EARLY else (outs[2 * i + 1], EARLY)
        out[k - first] = coded(buffer[at], field)


def packed(acc, base, tiles, source, lanes):
    for j, tile in enumerate(tiles):
        start = base + 4 * j
        moved = pltpu.roll(tile, lax.rem(start - source + 128, 128), 1)
        acc = jnp.where((lanes >= start) & (lanes < start + 4), moved, acc)
    return acc


def rows_kernel(now_hbm, prev_hbm, speed_hbm, up_ref, down_ref, buffer, sems):
    nz, nx, ny = now_hbm.shape
    copies = []
    for j, field in enumerate((now_hbm, prev_hbm, speed_hbm)):
        for i, begin in enumerate((nx - 8, 0)):
            copy = pltpu.make_async_copy(
                field.at[:, pl.ds(begin, 8), :], buffer.at[j, i], sems.at[j, i]
            )
            copy.start()
            copies.append(copy)
    for copy in copies:
        copy.wait()
    low = lax.broadcasted_iota(I32, (8, ny), 0) < 4
    for z in range(nz):
        up_ref[0, z] = jnp.where(low, pltpu.roll(buffer[1, 0, z], 4, 0), buffer[0, 0, z])
        up_ref[1, z] = buffer[2, 0, z]
        down_ref[0, z] = jnp.where(low, buffer[0, 1, z], pltpu.roll(buffer[1, 1, z], 4, 0))
        down_ref[1, z] = buffer[2, 1, z]


def ghost_rows(ref, z, top):
    pair, speed = ref[0, z], ref[1, z]
    keep = lax.broadcasted_iota(I32, pair.shape, 0) < 4
    keep = jnp.logical_not(keep) if top else keep
    return (
        jnp.where(keep, pair, 0.0),
        jnp.where(keep, pltpu.roll(pair, 4, 0), 0.0),
        jnp.where(keep, speed, 0.0),
    )


def columns_kernel(
    info_ref, now_hbm, prev_hbm, speed_hbm, top_ref, bottom_ref, left_ref, right_ref, buffer, sems
):
    nz, nx, ny = now_hbm.shape
    flip = info_ref[0]
    copies = []
    for z in range(nz):
        for j, field in enumerate((now_hbm, prev_hbm, speed_hbm)):
            copy = pltpu.make_async_copy(field.at[z], buffer.at[j, z], sems.at[j, z])
            copy.start()
            copies.append(copy)
    sides = ((left_ref, 0, 0), (right_ref, ny - 128, 124))
    lanes = lax.broadcasted_iota(I32, (8, 128), 1)
    for out, begin, source in sides:
        for ref, top, row in ((top_ref, True, 0), (bottom_ref, False, 8 + nx)):
            acc = jnp.zeros((8, 128), F32)
            for z in range(nz):
                base = GROUP * flipped(z, flip, nz)
                tiles = [v[:, begin : begin + 128] for v in ghost_rows(ref, z, top)]
                acc = packed(acc, base, tiles, source, lanes)
            out[row : row + 8, :] = acc
        out[8 : 8 + nx, :] = jnp.zeros((nx, 128), F32)
    rows = 64
    lanes = lax.broadcasted_iota(I32, (rows, 128), 1)
    for z in range(nz):
        for copy in copies[3 * z : 3 * z + 3]:
            copy.wait()
        base = GROUP * flipped(z, flip, nz)
        for k in range(nx // rows):
            at = slice(k * rows, (k + 1) * rows)
            to = slice(8 + k * rows, 8 + (k + 1) * rows)
            for ref, begin, source in sides:
                tiles = [buffer[j, z, at, begin : begin + 128] for j in range(3)]
                ref[to, :] = packed(ref[to, :], base, tiles, source, lanes)


def windows_kernel(nt, info_ref, left_ref, right_ref, from_left, from_right, top_ref, bottom_ref, own_ref, *outs):
    nz, ny = top_ref.shape[1], top_ref.shape[3]
    rows = left_ref.shape[0]
    step = 16
    lanes = lax.broadcasted_iota(I32, (step, 128), 1)
    inner = lanes & (GROUP - 1)

    def chunk(k, _):
        at = pl.ds(pl.multiple_of(k * step, step), step)
        parts = (from_left[at, :], left_ref[at, :], right_ref[at, :], from_right[at, :])
        windows = []
        for j in range(3):
            moved = [pltpu.roll(part, (4 * i - 4 * j) % 128, 1) for i, part in enumerate(parts)]
            window = jnp.where(
                inner < 4, moved[0], jnp.where(inner < 8, moved[1], jnp.where(inner < 12, moved[2], moved[3]))
            )
            own_ref[j, at, :] = window
            windows.append(window)
        for side, out in zip(sides_of(nt), outs):
            acc = jnp.zeros((step, 128), F32)
            for e, (field, g) in enumerate(edge_entries()):
                moved = pltpu.roll(windows[field], (GROUP * (e - own_plane(nt, side, g, nz))) % 128, 1)
                moved = moved * CODE_SCALES[field]
                acc = jnp.where((lanes >= GROUP * e) & (lanes < GROUP * (e + 1)), moved, acc)
            out[at, :] = jnp.round(acc).astype(I32).astype(I16)
        return 0

    lax.fori_loop(0, rows // step, chunk, 0, unroll=rows // step)
    for side, out in zip(sides_of(nt), outs):
        for e, (field, g) in enumerate(edge_entries()):
            z = flipped(own_plane(nt, side, g, nz), info_ref[0], nz)
            both = jnp.concatenate(
                [ghost_rows(top_ref, z, True)[field], ghost_rows(bottom_ref, z, False)[field]], axis=0
            )
            both = coded(both, field)
            for t in range(ny // 128):
                row = rows + (e * (ny // 128) + t) * 16
                out[row : row + 16, :] = both[:, t * 128 : (t + 1) * 128]


def sources_kernel(
    nt, info_ref, now_hbm, prev_hbm, speed_hbm, msg_hbm, top_ref, bottom_ref, own_ref, *rest
):
    a_ref, b_ref, c_ref, qa_ref, qb_ref, qc_ref, src, qsrc, load_sems, *node_scratch = rest
    nz, nx, ny = now_hbm.shape
    rows = nx + 2 * OFF
    lots = a_ref.shape[0] // rows
    flip = info_ref[0]

    erows = own_ref.shape[1]
    pltpu.make_async_copy(msg_hbm.at[:, pl.ds(0, 8), :], node_scratch[0], node_scratch[3].at[0]).start()
    loads = []
    for i, (field, ref) in enumerate(((now_hbm, a_ref), (prev_hbm, b_ref), (speed_hbm, c_ref))):
        for p in range(nz):
            copy = pltpu.make_async_copy(
                field.at[flipped(p, flip, nz)],
                ref.at[pl.ds(p * rows + OFF, nx), :],
                load_sems.at[i * nz + p],
            )
            copy.start()
            loads.append(copy)

    zero = jnp.zeros((rows, 128), F32)
    edge_zero = jnp.zeros((16, ny), F32)
    for ref in (a_ref, b_ref, c_ref):
        for p in range(lots):
            ref[p * rows : p * rows + 16, :] = edge_zero
            ref[p * rows + OFF + nx : (p + 1) * rows, :] = edge_zero
    if nt == 2:
        for ref in (a_ref, b_ref):
            for t in range(ny // 128):
                ref[(lots - 1) * rows : lots * rows, t * 128 : (t + 1) * 128] = zero
    for p in range(nz):
        z = flipped(p, flip, nz)
        for ref, low, high in zip(
            (a_ref, b_ref, c_ref), ghost_rows(top_ref, z, True), ghost_rows(bottom_ref, z, False)
        ):
            ref[p * rows + 8 : p * rows + 16, :] = low
            ref[p * rows + OFF + nx : p * rows + OFF + nx + 8, :] = high
    for j, ref in enumerate((qa_ref, qb_ref, qc_ref)):
        ref[8 : 8 + erows, 0:128] = own_ref[j]
        ref[0:8, 0:128] = jnp.zeros((8, 128), F32)
        ref[8 + erows :, 0:128] = jnp.zeros((rows - 8 - erows, 128), F32)
        ref[:, 128:256] = zero
    place_nodes = find_nodes(nx, ny, msg_hbm, src, qsrc, *node_scratch)

    def clear_source(k, _):
        src[pl.ds(pl.multiple_of(k * rows, 8), rows), :] = zero
        return 0

    lax.fori_loop(0, src.shape[0] // rows, clear_source, 0)
    for k in range(qsrc.shape[0] // rows):
        qsrc[k * rows : (k + 1) * rows, :] = zero
    place_nodes()
    for copy in loads:
        copy.wait()


def find_nodes(nx, ny, msg_hbm, src, qsrc, msg_ref, spots_ref, spots, in_sems):
    rows = nx + 2 * OFF
    flat = src.shape[0] // (2 * STEPS)
    senders = msg_hbm.shape[0]

    def first_row(at):
        return ((at >> 3) << 5) + (at & 7)

    def spot(word):
        return pl.ds(word >> 7, STEPS, stride=8)

    def msg_copy(r):
        return pltpu.make_async_copy(msg_hbm.at[:, pl.ds(8 * r, 8), :], msg_ref, in_sems.at[0])

    def spots_copy():
        return pltpu.make_async_copy(spots_ref, spots, in_sems.at[1])

    first_msg = msg_copy(0)
    def find_spots(whole):
        code = msg_ref[:, STEPS, :].astype(I32)
        p = code >> 18
        row = (code >> 9) & 511
        col = (code & 511) - 8
        index = lax.broadcasted_iota(I32, code.shape, 1)
        used = code != 0
        t = jnp.clip(col >> 7, 0, ny // 128 - 1)
        inside = used & (col >= 0) & (col < ny)
        spare = (index & 1) * flat + ((index >> 1) & 7)
        at = jnp.where(inside, t * flat + p * rows + row, spare)
        turn = (col - t * 128 - index) & 127
        clash = jnp.zeros(code.shape, I32)
        for j in range(1, BATCH):
            same = (at == pltpu.roll(at, j, 1)) & ((index & (BATCH - 1)) >= j) & (index < 2 * BATCH)
            clash = clash | jnp.where(same, 1, 0)
        word = (first_row(at) << 7) + turn
        spots_ref[0] = jnp.where(clash > 0, (first_row(spare) << 7) + turn, word)
        spots_ref[1] = word if whole else jnp.where((clash > 0) | (index >= 2 * BATCH), word, -1)
        low = col < 4
        qlane = GROUP * (p & 7) + jnp.where(low, col + 4, col - (ny - 4) + 8)
        spots_ref[2] = (first_row((p >> 3) * rows + row) << 7) + ((qlane - index) & 127)
        begin = jnp.where(jnp.max(clash, axis=1, keepdims=True) > 0, 0, 2 * BATCH)
        counts = msg_ref[:, STEPS + 1, :].astype(I32)
        nears = msg_ref[:, STEPS + 2, :].astype(I32)
        spots_ref[3] = jnp.where(index == 0, counts, jnp.where(index == 1, nears, begin))

    first_msg.wait()
    find_spots(False)
    spots_copy().start()
    lane = lax.broadcasted_iota(I32, (8, 128), 1)

    def share(d, k, turn):
        one = jnp.where(lane == k, msg_ref[d], 0.0)
        return pltpu.roll(one, turn, 1)[0:STEPS]

    def place_batch(d, first):
        words = [spots[0, d, k] for k in range(first, first + BATCH)]
        tile = msg_ref[d]
        values = [
            src[spot(word), :] + pltpu.roll(jnp.where(lane == first + k, tile, 0.0), word & 127, 1)[0:STEPS]
            for k, word in enumerate(words)
        ]
        for word, value in zip(words, values):
            src[spot(word), :] = value

    def place_first(d, _):
        place_batch(d, 0)
        return 0

    def place_second(i, _):
        group = [4 * i + j for j in range(4)]
        most = spots[3, group[0], 0]
        for d in group[1:]:
            most = jnp.maximum(most, spots[3, d, 0])

        @pl.when(most > BATCH)
        def _():
            for d in group:
                place_batch(d, BATCH)

        return 0

    def place_rest(r):
        def sender(d, most):
            count = spots[3, d, 0]

            def one(k, _):
                word = spots[1, d, k]

                @pl.when(word >= 0)
                def _():
                    src[spot(word), :] = src[spot(word), :] + share(d, k, word & 127)

                return 0

            def window(k, _):
                word = spots[2, d, k]
                qsrc[spot(word), :] = qsrc[spot(word), :] + share(d, k, word & 127)
                return 0

            first = 0 if r is not None else spots[3, d, 2]
            done = 0 if r is None else r * SLOTS
            lax.fori_loop(first, jnp.clip(count - done, 0, SLOTS), one, 0)
            lax.fori_loop(0, jnp.clip(spots[3, d, 1] - done, 0, SLOTS), window, 0)
            return jnp.maximum(most, count)

        return lax.fori_loop(0, senders, sender, 0)

    def place_nodes():
        spots_copy().wait()
        lax.fori_loop(0, senders, place_first, 0, unroll=8)
        lax.fori_loop(0, senders // 4, place_second, 0)
        most = place_rest(None)

        def extra(r, _):
            again = msg_copy(r)
            again.start()
            again.wait()
            find_spots(True)
            again = spots_copy()
            again.start()
            again.wait()
            place_rest(r)
            return 0

        lax.fori_loop(1, (most + SLOTS - 1) // SLOTS, extra, 0)

    return place_nodes


def steps_kernel(nt, info_ref, *rest):
    sides = sides_of(nt)
    n_side = len(sides)
    src, qsrc, rest = rest[6], rest[7], rest[8:]
    planes_in, rest = rest[:n_side], rest[n_side:]
    later_in, rest = rest[:n_side], rest[n_side:]
    edges_in, rest = rest[:n_side], rest[n_side:]
    out_prev, out_now, a_ref, b_ref, c_ref, qa_ref, qb_ref, qc_ref, store_sems = rest
    nz, nx, ny = out_now.shape
    rows = nx + 2 * OFF
    lots = a_ref.shape[0] // rows
    flat = src.shape[0] // (2 * STEPS)
    erows = nx + 16
    flip = info_ref[0]
    for side, planes, later, edges in zip(sides, planes_in, later_in, edges_in):
        for k, (field, g) in enumerate(z_entries(nz)):
            ref = (a_ref, b_ref, c_ref)[field]
            at = ghost_plane(side, g, nz) * rows
            ref[at + OFF : at + OFF + nx, :] = decoded(planes[k] if k < EARLY else later[k - EARLY], field)
        strip = edges[0:erows, :].astype(I32).astype(F32)
        lanes = lax.broadcasted_iota(I32, strip.shape, 1)
        for e, (field, g) in enumerate(edge_entries()):
            p = ghost_plane(side, g, nz)
            at = p * rows
            ref = (a_ref, b_ref, c_ref)[field]
            for t in range(ny // 128):
                row = erows + (e * (ny // 128) + t) * 16
                both = decoded(edges[row : row + 16, :], field)
                ref[at + 8 : at + 16, t * 128 : (t + 1) * 128] = both[0:8]
                ref[at + OFF + nx : at + OFF + nx + 8, t * 128 : (t + 1) * 128] = both[8:16]
            qref = (qa_ref, qb_ref, qc_ref)[field]
            lot = p - 8
            moved = pltpu.roll(strip, (GROUP * (lot - e)) % 128, 1) * (1.0 / CODE_SCALES[field])
            inside = (lanes >= GROUP * lot) & (lanes < GROUP * (lot + 1))
            qref[8 : 8 + erows, 128:256] = jnp.where(inside, moved, qref[8 : 8 + erows, 128:256])

    size = 16
    lanes = lax.broadcasted_iota(I32, (size, 128), 1)
    first, last = lanes == 0, lanes == 127

    def source_of(ref, at, s):
        return jnp.concatenate(
            [
                ref[pl.ds(pl.multiple_of((at + 8 * k) * STEPS + 8 * s, 8), 8), :]
                for k in range(size // 8)
            ],
            axis=0,
        )

    def main_step(s, now, prev, qnow, after=None):
        more = STEPS - 1 - s
        begin = OFF - 8 if more else OFF
        chunks = (nx + 16 if more else nx) // size

        def plane(i, _):
            p = i if nt == 2 else (i - more + lots) & (lots - 1)
            base = p * rows
            above = lax.rem(p + 1, lots) * rows
            below = lax.rem(p + lots - 1, lots) * rows
            qtile = pl.ds(pl.multiple_of((p >> 3) * 128, 128), 128)
            group = GROUP * (p & 7)
            to_first = lax.rem(256 - 3 - group, 128)
            to_last = lax.rem(256 + 127 - 12 - group, 128)

            def chunk(k, _):
                r0 = pl.multiple_of(begin + k * size, 8)

                def part(ref, at, t, extra=0):
                    at = pl.ds(pl.multiple_of(at + r0 - extra, 8), size + 2 * extra)
                    return ref[at, t * 128 : (t + 1) * 128]

                q = qnow[pl.ds(r0, size), qtile]
                mids = [part(now, base, t) for t in range(2)]
                ahead = [pltpu.roll(mid, 1, 1) for mid in mids]
                behind = [pltpu.roll(mid, 127, 1) for mid in mids]
                left = [
                    jnp.where(first, pltpu.roll(q, to_first, 1), ahead[0]),
                    jnp.where(first, ahead[0], ahead[1]),
                ]
                right = [
                    jnp.where(last, behind[1], behind[0]),
                    jnp.where(last, pltpu.roll(q, to_last, 1), behind[1]),
                ]
                for t in range(2):
                    wide = part(now, base, t, 8)
                    mid = mids[t]
                    beside = part(now, above, t) + part(now, below, t)
                    beside = beside + (wide[7 : 7 + size] + wide[9 : 9 + size])
                    beside = beside + (left[t] + right[t])
                    source = source_of(src, t * flat + base + r0, s)
                    result = (
                        2.0 * mid
                        - part(prev, base, t)
                        + (0.25 * part(c_ref, base, t)) * (beside - 6.0 * mid + source)
                    )
                    at = pl.ds(pl.multiple_of(base + r0, 8), size)
                    prev[at, t * 128 : (t + 1) * 128] = result
                return 0

            lax.fori_loop(0, chunks, chunk, 0, unroll=chunks)
            if after is not None:
                after(i)
            return 0

        lax.fori_loop(0, nz + n_side * more, plane, 0, unroll=True)

    def q_step(s, now, prev):
        def chunk(k, _):
            r0 = pl.multiple_of(OFF - 8 + k * size, 8)
            wide = now[pl.ds(pl.multiple_of(r0 - 8, 8), size + 16), :]
            mid = wide[8 : 8 + size]
            beside = wide[7 : 7 + size] + wide[9 : 9 + size]
            for shift in (1, 255, GROUP, 256 - GROUP):
                beside = beside + pltpu.roll(mid, shift, 1)
            at = pl.ds(r0, size)
            source = jnp.concatenate(
                [source_of(qsrc, r0, s), source_of(qsrc, rows + r0, s)], axis=1
            )
            prev[at, :] = (
                2.0 * mid
                - prev[at, :]
                + (0.25 * qc_ref[at, :]) * (beside - 6.0 * mid + source)
            )
            return 0

        lax.fori_loop(0, (nx + 16) // size, chunk, 0, unroll=(nx + 16) // size)

    fields, windows = [a_ref, b_ref], [qa_ref, qb_ref]

    def store(ref, out, p, sem):
        return pltpu.make_async_copy(
            ref.at[pl.ds(p * rows + OFF, nx), :], out.at[flipped(p, flip, nz)], sem
        )

    for s in range(STEPS - 1):
        main_step(s, fields[0], fields[1], windows[0])
        q_step(s, windows[0], windows[1])
        fields, windows = fields[::-1], windows[::-1]
    for p in range(nz):
        store(fields[0], out_prev, p, store_sems.at[p]).start()

    def finish(p):
        store(fields[1], out_now, p, store_sems.at[nz + p]).start()

    main_step(STEPS - 1, fields[0], fields[1], windows[0], finish)
    for p in range(nz):
        store(fields[0], out_prev, p, store_sems.at[p]).wait()
        store(fields[1], out_now, p, store_sems.at[nz + p]).wait()


def shifted(value, axis, count, step):
    pairs = [(i, i + step) for i in range(count) if 0 <= i + step < count]
    return lax.ppermute(value, axis, pairs)


def to_depth(values, nt):
    if nt == 2:
        return [lax.ppermute(values[0], "trace", [(0, 1), (1, 0)])]
    return [shifted(values[0], "trace", nt, -1), shifted(values[1], "trace", nt, 1)]


def body(traces, coupling, tap_shift, node_tile, node_cell, field_prev, field_now, speed_sq):
    nt, ngx, ngy = (lax.axis_size(axis) for axis in AXES)
    count = nt * ngx * ngy
    nodes = traces.shape[0]
    nz, nx, ny = field_now.shape
    sides = len(sides_of(nt))
    assert nz + 2 * STEPS == 16 and ny == 256
    shape = jax.ShapeDtypeStruct
    flip = lax.axis_index("trace") if nt == 2 else jnp.int32(0)
    info = jnp.full((1,), flip, I32)
    fields = (field_now, field_prev, speed_sq)

    entries = len(z_entries(nz))
    plane_msgs = call(
        functools.partial(planes_kernel, nt),
        [shape((EARLY, nx, ny), I16), shape((entries - EARLY, nx, ny), I16)] * sides,
        [smem_spec()] + [any_spec()] * 3,
        [vmem_spec()] * (2 * sides),
        [pltpu.VMEM((sides * entries, nx, ny), F32), pltpu.SemaphoreType.DMA((sides * entries,))],
        bytes_accessed=sides * entries * nx * ny * 6,
    )(info, *fields)
    planes = to_depth(plane_msgs[0::2], nt)

    up, down = call(
        rows_kernel,
        [shape((2, nz, 8, ny), F32)] * 2,
        [any_spec()] * 3,
        [vmem_spec()] * 2,
        [pltpu.VMEM((3, 2, nz, 8, ny), F32), pltpu.SemaphoreType.DMA((3, 2))],
        bytes_accessed=1 << 20,
    )(*fields)
    top = shifted(up, "gx", ngx, 1)
    bottom = shifted(down, "gx", ngx, -1)

    rounds = -(-nodes // SLOTS)
    ints = jnp.stack([tap_shift, node_tile[:, 0], node_cell])
    msg = call(
        functools.partial(amp_kernel, (nt, ngx, ngy, nz, nx, ny)),
        shape((count, 8 * rounds, SLOTS), F32),
        [any_spec(), vmem_spec(), vmem_spec(), any_spec()],
        vmem_spec(),
        [pltpu.VMEM((count, nodes), F32)] * 2
        + [pltpu.VMEM((count, SLOTS), F32)] * 2
        + [
            pltpu.VMEM(traces.shape, BF16),
            pltpu.VMEM((STEPS * RATE, NT), F32),
            pltpu.SemaphoreType.DMA((2,)),
        ],
        bytes_accessed=1 << 20,
        flops=1 << 30,
    )(*in_hbm(traces), coupling, ints, *in_hbm(jnp.asarray(sinc_table())))
    msg, top = lax.optimization_barrier((msg, top))
    msg = lax.all_to_all(msg, AXES, split_axis=0, concat_axis=0, tiled=True)

    erows = nx + 16
    left, right = call(
        columns_kernel,
        [shape((erows, 128), F32)] * 2,
        [smem_spec()] + [any_spec()] * 3 + [vmem_spec()] * 2,
        [vmem_spec()] * 2,
        [pltpu.VMEM((3, nz, nx, ny), F32), pltpu.SemaphoreType.DMA((3, nz))],
        bytes_accessed=3 * nz * nx * ny * 4,
    )(info, *fields, top, bottom)
    from_left = shifted(right, "gy", ngy, 1)
    from_right = shifted(left, "gy", ngy, -1)
    from_left, from_right, *later = lax.optimization_barrier(
        (from_left, from_right, *plane_msgs[1::2])
    )
    later = to_depth(later, nt)

    edge_rows = erows + len(edge_entries()) * (ny // 128) * 16
    own, *edge_msgs = call(
        functools.partial(windows_kernel, nt),
        [shape((3, erows, 128), F32)] + [shape((edge_rows, 128), I16)] * sides,
        [smem_spec()] + [vmem_spec()] * 6,
        [vmem_spec()] * (1 + sides),
        bytes_accessed=1 << 20,
    )(info, left, right, from_left, from_right, top, bottom)
    edges = to_depth(edge_msgs, nt)

    rows = nx + 2 * OFF
    lots = nz + STEPS + 1 if nt == 2 else nz + 2 * STEPS
    source_lots = nz + STEPS - 1 if nt == 2 else lots
    state = [pltpu.VMEM((lots * rows, ny), F32)] * 3 + [pltpu.VMEM((rows, 256), F32)] * 3
    sources = [
        pltpu.VMEM((2 * source_lots * rows * STEPS, 128), F32),
        pltpu.VMEM((2 * rows * STEPS, 128), F32),
    ]
    held = call(
        functools.partial(sources_kernel, nt),
        state + sources,
        [smem_spec()] + [any_spec()] * 4 + [vmem_spec()] * 3,
        [vmem_spec()] * 8,
        [
            pltpu.SemaphoreType.DMA((3 * nz,)),
            pltpu.VMEM((count, 8, SLOTS), F32),
            pltpu.VMEM((4, count, SLOTS), I32),
            pltpu.SMEM((4, count, SLOTS), I32),
            pltpu.SemaphoreType.DMA((2,)),
        ],
        bytes_accessed=4 * nz * nx * ny * 4,
        flops=nz * nx * ny * 16,
        limit=SMALL_LIMIT,
    )(info, *in_hbm(*fields, msg), top, bottom, own)
    out_prev, out_now, *_ = call(
        functools.partial(steps_kernel, nt),
        [shape((nz, nx, ny), F32)] * 2 + state,
        [smem_spec()] + [vmem_spec()] * (8 + 3 * sides),
        [any_spec()] * 2 + [vmem_spec()] * 6,
        [pltpu.SemaphoreType.DMA((2 * nz,))],
        bytes_accessed=5 * nz * nx * ny * 4,
        flops=nz * nx * ny * STEPS * 16,
        aliases={1 + i: 2 + i for i in range(6)},
        limit=SMALL_LIMIT,
    )(info, *held, *planes, *later, *edges)
    return out_prev, out_now


def solution(mesh):
    placed = (
        P(AXES, None, None),
        P(AXES, None),
        P(AXES),
        P(AXES, None),
        P(AXES),
        P("trace", "gx", "gy"),
        P("trace", "gx", "gy"),
        P("trace", "gx", "gy"),
    )
    return jax.shard_map(
        body,
        mesh=mesh,
        in_specs=placed,
        out_specs=(P("trace", "gx", "gy"), P("trace", "gx", "gy")),
        check_vma=False,
    )
```
